256 devices in a mesh: row: 16 (over z, y_lo), pair: 16 (over y_hi, x, core).
Axes of the slice: x: 4, y: 4 (y_hi: 2, y_lo: 2; y = y_hi * 2 + y_lo), z: 8, core: 2. Of those that a mesh axis runs over, the one named last changes fastest.
Arguments:
- slab: float32 [16384, 8192], P('row', 'pair'), may hold values from -400 to 400
- moves: int32 [1, 16], P(None, 'pair'), may hold values from 0 to 1, as said below
Outputs:
- rotated_slab: float32 [16384, 8192], P('row', 'pair')
The draws below stay inside these ranges and needn't reach their ends.
Inputs may be any that keep to these rules, and one draw needn't show every extreme that they name: Every row of moves holds both values.
All inputs are finite; a program needn't handle non-finite values.
Results may differ from the reference program's by a relative error of at most 0.0003.
Values sent between devices are 32-bit elements; how exact they have to be, the bound alone decides.
A program may use at most 64 MiB of HBM per device.

```python
import math
import jax
import jax.numpy as jnp
from jax import lax

B = 256
ITERS = 3
ROUNDS = 2
PAIRS = 16
ROWS = 16384
COLS = 8192


def draw_slab(key, part):
    key = jax.random.fold_in(key, 1)
    keys = jax.random.split(key, 3)
    row_scale = jnp.exp(jax.random.uniform(keys[0], (ROWS, 1), jnp.float32) * math.log(10.0))
    col_scale = jnp.exp(jax.random.uniform(keys[1], (1, COLS), jnp.float32) * math.log(10.0))
    entries = jnp.clip(jax.random.normal(keys[2], (ROWS, COLS), jnp.float32), -4.0, 4.0)
    return (entries * row_scale * col_scale).astype(jnp.float32)


def draw_moves(key, part):
    key = jax.random.fold_in(key, 7)
    keys = jax.random.split(key, 2)
    values = jax.random.randint(keys[0], (ROUNDS - 1, PAIRS), 0, 2)
    chosen = jax.random.randint(keys[1], (ROUNDS - 1, 1), 0, PAIRS)
    slots = jnp.arange(PAIRS)[None, :]
    neighbour = jnp.roll(values, -1, axis=1)
    values = jnp.where(slots == chosen, 1 - neighbour, values)
    return values.astype(jnp.int32)


def setup_inputs(seed: int = 0) -> dict:
    arg_keys = jax.random.split(jax.random.key(seed), 3)
    slab = draw_slab(jax.random.fold_in(arg_keys[2], 71), 0)
    moves = draw_moves(jax.random.fold_in(arg_keys[2], 71), 0)
    return {"slab": slab, "moves": moves}


epsilon = 1e-06

def product(left_side, right_side):
    return jnp.dot(left_side, right_side, precision=lax.Precision.HIGHEST, preferred_element_type=jnp.float32)

def gram_of(pair_block):
    return lax.dot_general(pair_block, pair_block, (((0,), (0,)), ((), ())), precision=lax.Precision.HIGHEST, preferred_element_type=jnp.float32)

def inverse_root(gram_full):
    width = gram_full.shape[0]
    gram_scale = jnp.sqrt(jnp.sum(gram_full * gram_full) + epsilon)
    powers = gram_full / gram_scale
    identity = jnp.eye(width, dtype=jnp.float32)
    inverse = identity
    for iteration in range(ITERS):
        if iteration == 0:
            tangent = 0.5 * (3.0 * identity - powers)
            inverse = tangent
        else:
            tangent = 0.5 * (3.0 * identity - product(inverse, powers))
            inverse = product(tangent, inverse)
        if iteration + 1 < ITERS:
            powers = product(tangent, powers)
    return (inverse, gram_scale)

def reference(slab, moves):
    blocks = jnp.transpose(slab.reshape(ROWS, PAIRS, 2 * B), (1, 0, 2))

    def rotate_pair(pair_block):
        inverse, gram_scale = inverse_root(gram_of(pair_block))
        return product(pair_block, inverse) * jnp.sqrt(ROWS / gram_scale)
    for round_index in range(ROUNDS):
        blocks = lax.map(rotate_pair, blocks)
        if round_index + 1 < ROUNDS:
            move_flag = moves[round_index][:, None, None]
            lead_block = blocks[:, :, :B]
            trail_block = blocks[:, :, B:]
            forward = jnp.where(move_flag == 0, lead_block, trail_block)
            backward = jnp.where(move_flag == 0, trail_block, lead_block)
            blocks = jnp.concatenate([jnp.roll(forward, 1, axis=0), jnp.roll(backward, -1, axis=0)], axis=2)
    return jnp.transpose(blocks, (1, 0, 2)).reshape(ROWS, PAIRS * 2 * B)
```

```python
import functools

import jax
import jax.numpy as jnp
from jax import lax
from jax.experimental import pallas as pl
from jax.experimental.pallas import tpu as pltpu
from jax.sharding import PartitionSpec as P

MESH = pl.DeviceIdType.MESH
F32 = jnp.float32
BF16 = jnp.bfloat16
N = 16
H = 256
W = 512
R = 1024
ROWS = 16384
EPS = 1e-06
T = 256
CHUNKS1 = (4, 3, 3)
CHUNKS2 = (2, 2)


def dot(a, b):
    return jnp.dot(a, b, preferred_element_type=F32)


def split(v):
    hi = v.astype(BF16)
    return hi, (v - hi.astype(F32)).astype(BF16)


def keep(ref, rows, v):
    hi, lo = split(v)
    ref[0, rows, :] = hi
    ref[1, rows, :] = lo


def product(a, rows, b, cols=slice(None)):
    ah, al = a[0, rows, :], a[1, rows, :]
    bh, bl = b[0, :, cols], b[1, :, cols]
    return dot(ah, bh) + (dot(ah, bl) + dot(al, bh))


def tiles(n):
    return [pl.ds(i * T, T) for i in range(n // T)]


def eye_tile(i):
    r = lax.broadcasted_iota(jnp.int32, (T, W), 0) + i * T
    c = lax.broadcasted_iota(jnp.int32, (T, W), 1)
    return jnp.where(r == c, 1.0, 0.0).astype(F32)


def newton_schulz(a, ah, a2, u, v, z2, z2h, yh, z):
    for rows in tiles(W):
        keep(ah, rows, a[rows, :])
    for rows in tiles(W):
        at = a[rows, :]
        sq = product(ah, rows, ah)
        a2[rows, :] = sq
        keep(u, rows, sq - 5.0 * at)
        keep(v, rows, sq - 4.0 * at)
    for i, rows in enumerate(tiles(W)):
        p = product(u, rows, v)
        t = (p + 7.0 * a2[rows, :] - 39.0 * a[rows, :] + 36.0 * eye_tile(i)) * 0.0625
        z2[rows, :] = t
        keep(z2h, rows, t)
    for rows in tiles(W):
        keep(yh, rows, product(z2h, rows, ah))
        keep(u, rows, product(z2h, rows, z2h))
    for rows in tiles(W):
        z[rows, :] = 1.5 * z2[rows, :] - 0.5 * product(u, rows, yh)


class Reduce:
    def __init__(self, r, nb, part, parts, whole, ss, rs, sa, ra):
        self.r, self.nb = r, nb
        self.part, self.parts, self.whole = part, parts, whole
        self.ss, self.rs, self.sa, self.ra = ss, rs, sa, ra

    def put(self, j, block):
        self.part[:, j] = block.reshape(N, 8, 128)

    def scatter(self):
        for d in ORDER:
            to = lax.rem(self.r + d, N)
            pltpu.make_async_remote_copy(
                src_ref=self.part.at[to],
                dst_ref=self.parts.at[N - d],
                send_sem=self.ss,
                recv_sem=self.rs,
                device_id={"row": to},
                device_id_type=MESH,
            ).start()

    def _all(self, src, dst, ss, rs):
        return pltpu.make_async_remote_copy(
            src_ref=src.at[pl.ds(1, N - 1)],
            dst_ref=dst.at[pl.ds(1, N - 1)],
            send_sem=ss,
            recv_sem=rs,
            device_id={"row": lax.rem(self.r + 1, N)},
            device_id_type=MESH,
        )

    def gather(self):
        self._all(self.part, self.parts, self.ss, self.rs).wait_recv()
        total = self.part[self.r]
        for d in range(1, N):
            total = total + self.parts[d]
        self.whole[self.r] = total
        for d in ORDER:
            to = lax.rem(self.r + d, N)
            pltpu.make_async_remote_copy(
                src_ref=self.whole.at[self.r],
                dst_ref=self.whole.at[self.r],
                send_sem=self.sa,
                recv_sem=self.ra,
                device_id={"row": to},
                device_id_type=MESH,
            ).start()

    def arrive(self):
        self._all(self.whole, self.whole, self.sa, self.ra).wait_recv()

    def get(self, j):
        return self.whole[:, j].reshape(128, 128)

    def drain(self):
        self._all(self.part, self.parts, self.ss, self.rs).wait_send()
        self._all(self.whole, self.whole, self.sa, self.ra).wait_send()


ORDER = (8, 7, 9, 6, 10, 5, 11, 4, 12, 3, 13, 2, 14, 1, 15)


def kernel(x_hbm, mv_ref, out_hbm, *refs):
    n_ar = len(CHUNKS1) + len(CHUNKS2)
    ar_bufs, refs = refs[: 3 * n_ar], refs[3 * n_ar :]
    (x, xh, xt, a, ah, a2, u, v, z2, z2h, yh, z, d_out, d_in,
     s_out, s_in, q_out, q_in, nh, qt, out,
     load_sem, out_sem, ss, rs, sa, ra, xs, xr) = refs
    r, p = lax.axis_index("row"), lax.axis_index("pair")
    odd = lax.rem(p, 2)
    slow = lax.rem(p + (N - 1) + 2 * odd, N)
    quick = p + 1 - 2 * odd

    loads = []
    for i, rows in enumerate(tiles(R)):
        c = pltpu.make_async_copy(x_hbm.at[rows], x.at[rows], load_sem.at[i])
        c.start()
        loads.append(c)
    barrier = pltpu.get_barrier_semaphore()
    for d in range(1, N):
        pl.semaphore_signal(
            barrier, inc=1, device_id={"row": lax.rem(r + d, N)}, device_id_type=MESH
        )
    for to in (slow, quick):
        pl.semaphore_signal(barrier, inc=1, device_id={"pair": to}, device_id_type=MESH)

    chunks = []
    for i, nb in enumerate(CHUNKS1 + CHUNKS2):
        chunks.append(
            Reduce(r, nb, *ar_bufs[3 * i : 3 * i + 3], ss.at[i], rs.at[i], sa.at[i], ra.at[i])
        )
    first, second = chunks[: len(CHUNKS1)], chunks[len(CHUNKS1) :]

    for i, rows in enumerate(tiles(R)):
        loads[i].wait()
        xv = x[rows, :]
        hi, lo = split(xv)
        xh[0, rows, :] = hi
        xh[1, rows, :] = lo
        xt[:, rows] = hi.astype(F32).T.astype(BF16)
    lead, trail = pl.ds(0, H), pl.ds(H, H)

    def mixed(i, j):
        return dot(xt[i, :], xh[1, :, j])

    def square(i, j):
        return dot(xt[i, :], xh[0, :, j])

    cross = square(lead, trail) + (mixed(lead, trail) + mixed(trail, lead).T)
    for j in range(4):
        i0, j0 = 128 * (j // 2), 128 * (j % 2)
        first[0].put(j, cross[i0 : i0 + 128, j0 : j0 + 128])
    pl.semaphore_wait(barrier, N + 1)
    first[0].scatter()
    for c, cols in ((1, lead), (2, trail)):
        m = mixed(cols, cols)
        g = square(cols, cols) + (m + m.T)
        first[c].put(0, g[:128, :128])
        first[c].put(1, g[:128, 128:])
        first[c].put(2, g[128:, 128:])
        first[c].scatter()
    for c in first:
        c.gather()

    sq = jnp.zeros((8, 128), F32)

    def norm(block, weight):
        return weight * jnp.sum((block * block).reshape(16, 8, 128), axis=0)

    first[0].arrive()
    for j in range(4):
        i0, j0 = 128 * (j // 2), 128 * (j % 2)
        b = first[0].get(j)
        sq = sq + norm(b, 2.0)
        a[i0 : i0 + 128, H + j0 : H + j0 + 128] = b
        a[H + j0 : H + j0 + 128, i0 : i0 + 128] = b.T
    for c, o in ((1, 0), (2, H)):
        first[c].arrive()
        b0, b1, b2 = (first[c].get(j) for j in range(3))
        sq = sq + norm(b0, 1.0) + norm(b1, 2.0) + norm(b2, 1.0)
        a[o : o + 128, o : o + 128] = b0
        a[o : o + 128, o + 128 : o + 256] = b1
        a[o + 128 : o + 256, o : o + 128] = b1.T
        a[o + 128 : o + 256, o + 128 : o + 256] = b2
    scale = jnp.sqrt(jnp.sum(sq, keepdims=True) + EPS)
    inv = 1.0 / scale
    for rows in tiles(W):
        a[rows, :] = a[rows, :] * inv
    newton_schulz(a, ah, a2, u, v, z2, z2h, yh, z)
    back = jnp.sqrt(ROWS / scale)

    lead_slow = (mv_ref[...] + odd) == 1
    for rows in tiles(W):
        zl, zt = z[rows, :H] * back, z[rows, H:] * back
        keep(u, rows, jnp.concatenate(
            [jnp.where(lead_slow, zl, zt), jnp.where(lead_slow, zt, zl)], axis=1))
        keep(z2h, rows, z[rows, :])

    def send(src, dst, i, to):
        c = pltpu.make_async_remote_copy(
            src_ref=src, dst_ref=dst, send_sem=xs.at[i], recv_sem=xr.at[i],
            device_id={"pair": to}, device_id_type=MESH,
        )
        c.start()
        return c

    for rows in tiles(R):
        t = product(xh, rows, u, lead)
        s_out[0, rows, :] = t[:, :128]
        s_out[1, rows, :] = t[:, 128:]
    s_sent = [send(s_out.at[c], s_in.at[c], c, slow) for c in range(2)]
    for rows in tiles(R):
        q_out[rows, :] = product(xh, rows, u, trail)
    q_sent = send(q_out, q_in, 2, quick)

    for rows in tiles(W):
        keep(v, rows, product(z2h, rows, ah))
    dl, dt = product(z2h, lead, v, lead), product(z2h, trail, v, trail)
    d_out[0] = jnp.where(lead_slow, dl, dt) * float(ROWS)
    d_out[1] = jnp.where(lead_slow, dt, dl) * float(ROWS)
    d_sent = [send(d_out.at[i], d_in.at[i], 3 + i, to) for i, to in ((0, slow), (1, quick))]

    q_sent.wait_recv()
    for rows in tiles(R):
        hi, lo = split(q_in[rows, :])
        nh[0, rows, H:] = hi
        nh[1, rows, H:] = lo
        qt[0, :, rows] = hi.astype(F32).T.astype(BF16)
        qt[1, :, rows] = lo.astype(F32).T.astype(BF16)
    for c in range(2):
        cols = pl.ds(128 * c, 128)
        s_sent[c].wait_recv()
        for rows in tiles(R):
            hi, lo = split(s_in[c, rows, :])
            nh[0, rows, cols] = hi
            nh[1, rows, cols] = lo
        g = dot(qt[0], nh[0, :, cols]) + (dot(qt[0], nh[1, :, cols]) + dot(qt[1], nh[0, :, cols]))
        second[c].put(0, g[:128])
        second[c].put(1, g[128:])
        second[c].scatter()
    for c in second:
        c.gather()
    for c in d_sent:
        c.wait_recv()
    sq = jnp.zeros((8, 128), F32)
    for i, o in ((0, 0), (1, H)):
        for rows in range(0, H, 128):
            b = d_in[i, rows : rows + 128, :]
            sq = sq + norm(b[:, :128], 1.0) + norm(b[:, 128:], 1.0)
            a[o + rows : o + rows + 128, o : o + H] = b
    for c in range(2):
        second[c].arrive()
        for j in range(2):
            b = second[c].get(j)
            sq = sq + norm(b, 2.0)
            i0, j0 = H + 128 * j, 128 * c
            a[i0 : i0 + 128, j0 : j0 + 128] = b
            a[j0 : j0 + 128, i0 : i0 + 128] = b.T
    scale = jnp.sqrt(jnp.sum(sq, keepdims=True) + EPS)
    inv = 1.0 / scale
    for rows in tiles(W):
        a[rows, :] = a[rows, :] * inv
    newton_schulz(a, ah, a2, u, v, z2, z2h, yh, z)
    back = jnp.sqrt(ROWS / scale)
    for rows in tiles(W):
        keep(u, rows, z[rows, :] * back)
    s_cols = pl.ds(pl.multiple_of(odd * H, H), H)
    q_cols = pl.ds(pl.multiple_of((1 - odd) * H, H), H)
    stores = []
    for i, rows in enumerate(tiles(R)):
        t = product(nh, rows, u)
        out[0, rows, :] = t[:, :H]
        out[1, rows, :] = t[:, H:]
        for k, cols in ((0, s_cols), (1, q_cols)):
            c = pltpu.make_async_copy(
                out.at[k, rows], out_hbm.at[rows, cols], out_sem.at[2 * i + k]
            )
            c.start()
            stores.append(c)
    for c in s_sent + [q_sent] + d_sent:
        c.wait_send()
    for c in chunks:
        c.drain()
    for c in stores:
        c.wait()


def local(slab, moves):
    ar = []
    for nb in CHUNKS1 + CHUNKS2:
        ar += [pltpu.VMEM((N, nb, 8, 128), F32)] * 3
    n_ar = len(CHUNKS1) + len(CHUNKS2)
    half = lambda *s: pltpu.VMEM(s, BF16)
    full = lambda *s: pltpu.VMEM(s, F32)
    return pl.pallas_call(
        kernel,
        out_shape=jax.ShapeDtypeStruct((R, W), F32),
        in_specs=[
            pl.BlockSpec(memory_space=pl.ANY),
            pl.BlockSpec(memory_space=pltpu.VMEM),
        ],
        out_specs=pl.BlockSpec(memory_space=pl.ANY),
        scratch_shapes=ar
        + [
            full(R, W), half(2, R, W), half(W, R),
            full(W, W), half(2, W, W), full(W, W), half(2, W, W), half(2, W, W),
            full(W, W), half(2, W, W), half(2, W, W), full(W, W),
            full(2, H, H), full(2, H, H),
            full(2, R, 128), full(2, R, 128), full(R, H), full(R, H),
            half(2, R, W), half(2, H, R), full(2, R, H),
            pltpu.SemaphoreType.DMA((4,)),
            pltpu.SemaphoreType.DMA((8,)),
            pltpu.SemaphoreType.DMA((n_ar,)),
            pltpu.SemaphoreType.DMA((n_ar,)),
            pltpu.SemaphoreType.DMA((n_ar,)),
            pltpu.SemaphoreType.DMA((n_ar,)),
            pltpu.SemaphoreType.DMA((5,)),
            pltpu.SemaphoreType.DMA((5,)),
        ],
        compiler_params=pltpu.CompilerParams(
            collective_id=1, has_side_effects=True, vmem_limit_bytes=50 * 2**20
        ),
    )(slab, moves)


def solution(mesh):
    placed = (P("row", "pair"), P(None, "pair"))
    return jax.shard_map(
        local, mesh=mesh, in_specs=placed, out_specs=P("row", "pair"), check_vma=False
    )
```

```python
import functools

import jax
import jax.numpy as jnp
from jax import lax
from jax.experimental import pallas as pl
from jax.experimental.pallas import tpu as pltpu
from jax.sharding import PartitionSpec as P

MESH = pl.DeviceIdType.MESH
F32 = jnp.float32
BF16 = jnp.bfloat16
N = 16
H = 256
W = 512
R = 1024
ROWS = 16384
EPS = 1e-06
T = 256
CHUNKS1 = ((2, 0), (2, 0), (2, 0), (2, 2))
CHUNKS2 = (2, 2)


def dot(a, b):
    return jnp.dot(a, b, preferred_element_type=F32)


def split(v):
    hi = v.astype(BF16)
    return hi, (v - hi.astype(F32)).astype(BF16)


def keep(ref, rows, v):
    hi, lo = split(v)
    ref[0, rows, :] = hi
    ref[1, rows, :] = lo


def product(a, rows, b, cols=slice(None)):
    ah, al = a[0, rows, :], a[1, rows, :]
    bh, bl = b[0, :, cols], b[1, :, cols]
    return dot(ah, bh) + (dot(ah, bl) + dot(al, bh))


def tiles(n):
    return [pl.ds(i * T, T) for i in range(n // T)]


def eye_tile(i):
    r = lax.broadcasted_iota(jnp.int32, (T, W), 0) + i * T
    c = lax.broadcasted_iota(jnp.int32, (T, W), 1)
    return jnp.where(r == c, 1.0, 0.0).astype(F32)


def symmetric(a, b):
    top = product(a, pl.ds(0, H), b)
    low = product(a, pl.ds(H, H), b, pl.ds(H, H))
    return top, jnp.concatenate([top[:, H:].T, low], axis=1)


def newton_schulz(a, ah, a2, u, v, z2, z2h, yh):
    for rows in tiles(W):
        keep(ah, rows, a[rows, :])
    for rows, sq in zip(tiles(W), symmetric(ah, ah)):
        at = a[rows, :]
        a2[rows, :] = sq
        keep(u, rows, sq - 5.0 * at)
        keep(v, rows, sq - 4.0 * at)
    for i, (rows, p) in enumerate(zip(tiles(W), symmetric(u, v))):
        t = (p + 7.0 * a2[rows, :] - 39.0 * a[rows, :] + 36.0 * eye_tile(i)) * 0.0625
        z2[rows, :] = t
        keep(z2h, rows, t)
    for rows, y in zip(tiles(W), symmetric(z2h, ah)):
        keep(yh, rows, y)
    for rows, t in zip(tiles(W), symmetric(z2h, z2h)):
        keep(u, rows, t)


class Reduce:
    def __init__(self, r, nb, part, parts, whole, ss, rs, sa, ra):
        self.r, self.nb = r, nb
        self.part, self.parts, self.whole = part, parts, whole
        self.ss, self.rs, self.sa, self.ra = ss, rs, sa, ra

    def put(self, j, block):
        self.part[:, j] = block.reshape(N, 8, 128)

    def scatter(self):
        for d in ORDER:
            to = lax.rem(self.r + d, N)
            pltpu.make_async_remote_copy(
                src_ref=self.part.at[to],
                dst_ref=self.parts.at[N - d],
                send_sem=self.ss,
                recv_sem=self.rs,
                device_id={"row": to},
                device_id_type=MESH,
            ).start()

    def _all(self, src, dst, ss, rs):
        return pltpu.make_async_remote_copy(
            src_ref=src.at[pl.ds(1, N - 1)],
            dst_ref=dst.at[pl.ds(1, N - 1)],
            send_sem=ss,
            recv_sem=rs,
            device_id={"row": lax.rem(self.r + 1, N)},
            device_id_type=MESH,
        )

    def gather(self):
        self._all(self.part, self.parts, self.ss, self.rs).wait_recv()
        total = self.part[self.r]
        for d in range(1, N):
            total = total + self.parts[d]
        self.whole[self.r] = total
        for d in ORDER:
            to = lax.rem(self.r + d, N)
            pltpu.make_async_remote_copy(
                src_ref=self.whole.at[self.r],
                dst_ref=self.whole.at[self.r],
                send_sem=self.sa,
                recv_sem=self.ra,
                device_id={"row": to},
                device_id_type=MESH,
            ).start()

    def arrive(self):
        self._all(self.whole, self.whole, self.sa, self.ra).wait_recv()

    def get(self, j):
        return self.whole[:, j].reshape(128, 128)

    def drain(self):
        self._all(self.part, self.parts, self.ss, self.rs).wait_send()
        self._all(self.whole, self.whole, self.sa, self.ra).wait_send()


class Fold:
    def __init__(self, r, nb, part, yb, half, zb, whole, ss, rs):
        self.r, self.z, self.y = r, r // 2, lax.rem(r, 2)
        self.other = r + 1 - 2 * self.y
        self.nb = nb
        self.part, self.yb, self.half, self.zb, self.whole = part, yb, half, zb, whole
        self.ss, self.rs = ss, rs

    def put(self, j, block):
        self.part[:, :, 8 * j : 8 * j + 8, :] = block.reshape(2, 8, 8, 128)

    def put_rows(self, rows):
        at = 8 * self.nb
        self.part[:, :, at : at + 2, :] = jnp.zeros((2, 8, 2, 128), F32)
        self.part[0, 0, at : at + 2, :] = rows

    def copy(self, src, dst, i, row):
        return pltpu.make_async_remote_copy(
            src_ref=src, dst_ref=dst, send_sem=self.ss.at[i], recv_sem=self.rs.at[i],
            device_id={"row": row}, device_id_type=MESH,
        )

    def over_y(self):
        return self.copy(self.part.at[1 - self.y], self.yb, 0, self.other)

    def seven(self, i):
        return self.copy(self.half.at[pl.ds(1, 7)], self.zb.at[pl.ds(1, 7)], i, self.other)

    def back_y(self):
        mine = self.whole.at[self.y]
        return self.copy(mine, mine, 3, self.other)

    def scatter_y(self):
        self.over_y().start()

    def scatter_z(self):
        self.over_y().wait_recv()
        self.half[...] = self.part[self.y] + self.yb[...]
        for d in ORDER_Z:
            to = lax.rem(self.z + d, 8)
            self.copy(self.half.at[to], self.zb.at[8 - d], 1, to * 2 + self.y).start()

    def gather_z(self):
        self.seven(1).wait_recv()
        total = self.half[self.z]
        for d in range(1, 8):
            total = total + self.zb[d]
        self.whole[self.y, self.z] = total
        mine = self.whole.at[self.y, self.z]
        for d in ORDER_Z:
            self.copy(mine, mine, 2, lax.rem(self.z + d, 8) * 2 + self.y).start()

    def gather_y(self):
        self.seven(2).wait_recv()
        self.back_y().start()

    def arrive(self):
        self.back_y().wait_recv()

    def get(self, j):
        return self.whole[:, :, 8 * j : 8 * j + 8, :].reshape(128, 128)

    def get_row(self, k):
        at = 8 * self.nb + k
        return self.whole[0, 0, at : at + 1, :]

    def drain(self):
        self.over_y().wait_send()
        self.seven(1).wait_send()
        self.seven(2).wait_send()
        self.back_y().wait_send()


ORDER_Z = (4, 3, 5, 2, 6, 1, 7)
ORDER = (8, 7, 9, 6, 10, 5, 11, 4, 12, 3, 13, 2, 14, 1, 15)


def upper():
    r = lax.broadcasted_iota(jnp.int32, (128, 128), 0)
    c = lax.broadcasted_iota(jnp.int32, (128, 128), 1)
    return r < c, r == c


def norm(block, weight):
    return weight * jnp.sum((block * block).reshape(-1, 8, block.shape[1]), axis=0)


def kernel(x_hbm, mv_ref, out_hbm, *refs):
    n1, n2 = len(CHUNKS1), len(CHUNKS2)
    bufs1, refs = refs[: 5 * n1], refs[5 * n1 :]
    bufs2, refs = refs[: 3 * n2], refs[3 * n2 :]
    (x, xh, xt, a, ah, a2, u, v, z2, z2h, yh, zh, d_out, d_in,
     s_out, s_in, q_out, q_in, nh, qt, out,
     load_sem, out_sem, ss1, rs1, ss2, rs2, xs, xr) = refs
    r, p = lax.axis_index("row"), lax.axis_index("pair")
    odd = lax.rem(p, 2)
    slow = lax.rem(p + (N - 1) + 2 * odd, N)
    quick = p + 1 - 2 * odd
    first = [
        Fold(r, nb, *bufs1[5 * i : 5 * i + 5], ss1.at[i], rs1.at[i])
        for i, (nb, _) in enumerate(CHUNKS1)
    ]
    second = [
        Reduce(r, nb, *bufs2[3 * i : 3 * i + 3], ss2.at[2 * i], rs2.at[2 * i], ss2.at[2 * i + 1], rs2.at[2 * i + 1])
        for i, nb in enumerate(CHUNKS2)
    ]

    loads = []
    for i, rows in enumerate(tiles(R)):
        c = pltpu.make_async_copy(x_hbm.at[rows], x.at[rows], load_sem.at[i])
        c.start()
        loads.append(c)
    barrier = pltpu.get_barrier_semaphore()
    for d in range(1, N):
        pl.semaphore_signal(
            barrier, inc=1, device_id={"row": lax.rem(r + d, N)}, device_id_type=MESH
        )
    for to in (slow, quick):
        pl.semaphore_signal(barrier, inc=1, device_id={"pair": to}, device_id_type=MESH)

    lead_slow = (mv_ref[...] + odd) == 1
    for i, rows in enumerate(tiles(R)):
        loads[i].wait()
        xl, xr_ = x[rows, :H], x[rows, H:]
        hi, lo = split(jnp.concatenate(
            [jnp.where(lead_slow, xl, xr_), jnp.where(lead_slow, xr_, xl)], axis=1))
        xh[0, rows, :] = hi
        xh[1, rows, :] = lo
        xt[:, rows] = hi.astype(F32).T.astype(BF16)
    sc, qc = pl.ds(0, H), pl.ds(H, H)

    def mixed(i, j):
        return dot(xt[i, :], xh[1, :, j])

    def square(i, j):
        return dot(xt[i, :], xh[0, :, j])

    cross = square(sc, qc) + (mixed(sc, qc) + mixed(qc, sc).T)
    for j in range(4):
        i0, j0 = 128 * (j // 2), 128 * (j % 2)
        first[j // 2].put(j % 2, cross[i0 : i0 + 128, j0 : j0 + 128])
    pl.semaphore_wait(barrier, N + 1)
    first[0].scatter_y()
    first[1].scatter_y()
    above, on = upper()
    packed, diagonal = [], []
    for c, cols in enumerate((sc, qc)):
        m = mixed(cols, cols)
        g = square(cols, cols) + (m + m.T)
        first[2].put(c, g[:128, 128:])
        low = g[128:, 128:]
        first[3].put(c, jnp.where(above | on, g[:128, :128], low))
        diagonal.append(jnp.sum(jnp.where(on, low, 0.0), axis=0, keepdims=True))
    first[3].put_rows(jnp.concatenate(diagonal, axis=0))
    first[2].scatter_y()
    first[3].scatter_y()
    for c in first:
        c.scatter_z()
    for c in first:
        c.gather_z()
    for c in first:
        c.gather_y()

    sq = jnp.zeros((8, 128), F32)
    for j in range(4):
        if j % 2 == 0:
            first[j // 2].arrive()
        i0, j0 = 128 * (j // 2), 128 * (j % 2)
        b = first[j // 2].get(j % 2)
        sq = sq + norm(b, 2.0)
        a[i0 : i0 + 128, H + j0 : H + j0 + 128] = b
        a[H + j0 : H + j0 + 128, i0 : i0 + 128] = b.T
    first[2].arrive()
    for c, o in ((0, 0), (1, H)):
        b = first[2].get(c)
        sq = sq + norm(b, 2.0)
        a[o : o + 128, o + 128 : o + 256] = b
        a[o + 128 : o + 256, o : o + 128] = b.T
    first[3].arrive()
    for c, o in ((0, 0), (1, H)):
        b = first[3].get(c)
        t = b.T
        b0 = jnp.where(above | on, b, t)
        b2 = jnp.where(above, t, jnp.where(on, first[3].get_row(c), b))
        sq = sq + norm(b0, 1.0) + norm(b2, 1.0)
        a[o : o + 128, o : o + 128] = b0
        a[o + 128 : o + 256, o + 128 : o + 256] = b2
    scale = jnp.sqrt(jnp.sum(sq, keepdims=True) + EPS)
    inv = 1.0 / scale
    for rows in tiles(W):
        a[rows, :] = a[rows, :] * inv
    newton_schulz(a, ah, a2, u, v, z2, z2h, yh)
    back = jnp.sqrt(ROWS / scale)

    def send(src, dst, i, to):
        c = pltpu.make_async_remote_copy(
            src_ref=src, dst_ref=dst, send_sem=xs.at[i], recv_sem=xr.at[i],
            device_id={"pair": to}, device_id_type=MESH,
        )
        c.start()
        return c

    top = 1.5 * z2[sc, :] - 0.5 * product(u, sc, yh)
    left = top[:, H:].T
    hi, lo = split(top[:, :H] * back)
    zh[0, sc, sc], zh[1, sc, sc] = hi, lo
    hi, lo = split(left * back)
    zh[0, qc, sc], zh[1, qc, sc] = hi, lo
    s_sent = [[], []]
    for i, rows in enumerate(tiles(R)):
        t = product(xh, rows, zh, sc)
        s_out[0, rows, :] = t[:, :128]
        s_out[1, rows, :] = t[:, 128:]
        s_sent[0].append(send(s_out.at[0, rows], s_in.at[0, rows], i, slow))
    for i, rows in enumerate(tiles(R)):
        s_sent[1].append(send(s_out.at[1, rows], s_in.at[1, rows], 4 + i, slow))
    low = 1.5 * z2[qc, qc] - 0.5 * product(u, qc, yh, qc)
    hi, lo = split(top[:, H:] * back)
    zh[0, sc, qc], zh[1, sc, qc] = hi, lo
    hi, lo = split(low * back)
    zh[0, qc, qc], zh[1, qc, qc] = hi, lo
    for rows in tiles(R):
        q_out[rows, :] = product(xh, rows, zh, qc)
    q_sent = send(q_out, q_in, 8, quick)

    keep(z2h, sc, top)
    keep(z2h, qc, jnp.concatenate([left, low], axis=1))
    for rows, t in zip(tiles(W), symmetric(z2h, ah)):
        keep(v, rows, t)
    d_out[0] = product(z2h, sc, v, sc) * float(ROWS)
    d_out[1] = product(z2h, qc, v, qc) * float(ROWS)
    d_sent = [send(d_out.at[i], d_in.at[i], 9 + i, to) for i, to in ((0, slow), (1, quick))]

    q_sent.wait_recv()
    for rows in tiles(R):
        hi, lo = split(q_in[rows, :])
        nh[0, rows, H:] = hi
        nh[1, rows, H:] = lo
        qt[0, :, rows] = hi.astype(F32).T.astype(BF16)
        qt[1, :, rows] = lo.astype(F32).T.astype(BF16)
    for c in range(2):
        cols = pl.ds(128 * c, 128)
        for i, rows in enumerate(tiles(R)):
            s_sent[c][i].wait_recv()
            hi, lo = split(s_in[c, rows, :])
            nh[0, rows, cols] = hi
            nh[1, rows, cols] = lo
        g = dot(qt[0], nh[0, :, cols]) + (dot(qt[0], nh[1, :, cols]) + dot(qt[1], nh[0, :, cols]))
        second[c].put(0, g[:128])
        second[c].put(1, g[128:])
        second[c].scatter()
    for c in second:
        c.gather()
    for c in d_sent:
        c.wait_recv()
    sq = jnp.zeros((8, 128), F32)
    for i, o in ((0, 0), (1, H)):
        for rows in range(0, H, 128):
            b = d_in[i, rows : rows + 128, :]
            sq = sq + norm(b[:, :128], 1.0) + norm(b[:, 128:], 1.0)
            a[o + rows : o + rows + 128, o : o + H] = b
    for c in range(2):
        second[c].arrive()
        for j in range(2):
            b = second[c].get(j)
            sq = sq + norm(b, 2.0)
            i0, j0 = H + 128 * j, 128 * c
            a[i0 : i0 + 128, j0 : j0 + 128] = b
            a[j0 : j0 + 128, i0 : i0 + 128] = b.T
    scale = jnp.sqrt(jnp.sum(sq, keepdims=True) + EPS)
    inv = 1.0 / scale
    for rows in tiles(W):
        a[rows, :] = a[rows, :] * inv
    newton_schulz(a, ah, a2, u, v, z2, z2h, yh)
    back = jnp.sqrt(ROWS / scale)
    top = (1.5 * z2[sc, :] - 0.5 * product(u, sc, yh)) * back
    low = (1.5 * z2[qc, qc] - 0.5 * product(u, qc, yh, qc)) * back
    keep(zh, sc, top)
    keep(zh, qc, jnp.concatenate([top[:, H:].T, low], axis=1))
    s_cols = pl.ds(pl.multiple_of(odd * H, H), H)
    q_cols = pl.ds(pl.multiple_of((1 - odd) * H, H), H)
    stores = []
    for i, rows in enumerate(tiles(R)):
        t = product(nh, rows, zh)
        out[0, rows, :] = t[:, :H]
        out[1, rows, :] = t[:, H:]
        for k, cols in ((0, s_cols), (1, q_cols)):
            c = pltpu.make_async_copy(
                out.at[k, rows], out_hbm.at[rows, cols], out_sem.at[2 * i + k]
            )
            c.start()
            stores.append(c)
    for c in s_sent[0] + s_sent[1] + [q_sent] + d_sent:
        c.wait_send()
    for c in first + second:
        c.drain()
    for c in stores:
        c.wait()


def local(slab, moves):
    half = lambda *s: pltpu.VMEM(s, BF16)
    full = lambda *s: pltpu.VMEM(s, F32)
    bufs = []
    for nb, more in CHUNKS1:
        t = (8 * nb + more, 128)
        bufs += [full(2, 8, *t), full(8, *t), full(8, *t), full(8, *t), full(2, 8, *t)]
    for nb in CHUNKS2:
        bufs += [full(N, nb, 8, 128)] * 3
    dma = lambda *n: pltpu.SemaphoreType.DMA(n)
    n1, n2 = len(CHUNKS1), len(CHUNKS2)
    return pl.pallas_call(
        kernel,
        out_shape=jax.ShapeDtypeStruct((R, W), F32),
        in_specs=[
            pl.BlockSpec(memory_space=pl.ANY),
            pl.BlockSpec(memory_space=pltpu.VMEM),
        ],
        out_specs=pl.BlockSpec(memory_space=pl.ANY),
        scratch_shapes=bufs
        + [
            full(R, W), half(2, R, W), half(W, R),
            full(W, W), half(2, W, W), full(W, W), half(2, W, W), half(2, W, W),
            full(W, W), half(2, W, W), half(2, W, W), half(2, W, W),
            full(2, H, H), full(2, H, H),
            full(2, R, 128), full(2, R, 128), full(R, H), full(R, H),
            half(2, R, W), half(2, H, R), full(2, R, H),
            dma(4), dma(8), dma(n1, 4), dma(n1, 4), dma(2 * n2), dma(2 * n2), dma(11), dma(11),
        ],
        compiler_params=pltpu.CompilerParams(
            collective_id=1, has_side_effects=True, vmem_limit_bytes=50 * 2**20
        ),
    )(slab, moves)


def solution(mesh):
    placed = (P("row", "pair"), P(None, "pair"))
    return jax.shard_map(
        local, mesh=mesh, in_specs=placed, out_specs=P("row", "pair"), check_vma=False
    )
```

```python
import functools

import jax
import jax.numpy as jnp
from jax import lax
from jax.experimental import pallas as pl
from jax.experimental.pallas import tpu as pltpu
from jax.sharding import PartitionSpec as P

MESH = pl.DeviceIdType.MESH
F32 = jnp.float32
BF16 = jnp.bfloat16
N = 16
H = 256
W = 512
R = 1024
ROWS = 16384
EPS = 1e-06
T = 256
CHUNKS1 = ((2, 0), (2, 0), (2, 0), (2, 2))
CHUNKS2 = (2, 1, 1)


def dot(a, b):
    return jnp.dot(a, b, preferred_element_type=F32)


def split(v):
    hi = v.astype(BF16)
    return hi, (v - hi.astype(F32)).astype(BF16)


def keep(ref, rows, v, cols=slice(None)):
    hi, lo = split(v)
    ref[0, rows, cols] = hi
    ref[1, rows, cols] = lo


def product(a, rows, b, cols=slice(None)):
    ah, al = a[0, rows, :], a[1, rows, :]
    bh, bl = b[0, :, cols], b[1, :, cols]
    return dot(ah, bh) + (dot(ah, bl) + dot(al, bh))


def tiles(n):
    return [pl.ds(i * T, T) for i in range(n // T)]


def eye_tile(i):
    r = lax.broadcasted_iota(jnp.int32, (T, W), 0) + i * T
    c = lax.broadcasted_iota(jnp.int32, (T, W), 1)
    return jnp.where(r == c, 1.0, 0.0).astype(F32)


def symmetric(a, b):
    top = product(a, pl.ds(0, H), b)
    low = product(a, pl.ds(H, H), b, pl.ds(H, H))
    return top, jnp.concatenate([top[:, H:].T, low], axis=1)


def newton_schulz(a, ah, inv, a2, u, v, z2, z2h, yh):
    for rows in tiles(W):
        keep(ah, rows, a[rows, :])
    inv2 = inv * inv
    for rows, sq in zip(tiles(W), symmetric(ah, ah)):
        at = a[rows, :] * inv
        a[rows, :] = at
        sq = sq * inv2
        a2[rows, :] = sq
        keep(u, rows, sq - 5.0 * at)
        keep(v, rows, sq - 4.0 * at)
    for i, (rows, p) in enumerate(zip(tiles(W), symmetric(u, v))):
        t = (p + 7.0 * a2[rows, :] - 39.0 * a[rows, :] + 36.0 * eye_tile(i)) * 0.0625
        z2[rows, :] = t
        keep(z2h, rows, t)
    for rows, y in zip(tiles(W), symmetric(z2h, ah)):
        keep(yh, rows, y * inv)
    for rows, t in zip(tiles(W), symmetric(z2h, z2h)):
        keep(u, rows, t)


class Line:
    def __init__(self, r, nb, part, parts, mine, theirs, whole, ss, rs):
        self.r, self.z, self.y = r, r // 2, lax.rem(r, 2)
        self.other = r + 1 - 2 * self.y
        self.part, self.parts, self.mine, self.theirs, self.whole = part, parts, mine, theirs, whole
        self.ss, self.rs = ss, rs

    def put(self, j, block):
        self.part[:, j] = block.reshape(8, 16, 128)

    def copy(self, src, dst, i, row):
        return pltpu.make_async_remote_copy(
            src_ref=src, dst_ref=dst, send_sem=self.ss.at[i], recv_sem=self.rs.at[i],
            device_id={"row": row}, device_id_type=MESH,
        )

    def seven(self, i):
        return self.copy(self.part.at[pl.ds(1, 7)], self.parts.at[pl.ds(1, 7)], i, self.other)

    def over_y(self):
        return self.copy(self.mine, self.theirs, 1, self.other)

    def scatter(self):
        for d in ORDER_Z:
            to = lax.rem(self.z + d, 8)
            self.copy(self.part.at[to], self.parts.at[8 - d], 0, to * 2 + self.y).start()

    def swap(self):
        self.seven(0).wait_recv()
        total = self.part[self.z]
        for d in range(1, 8):
            total = total + self.parts[d]
        self.mine[...] = total
        self.over_y().start()

    def gather(self):
        self.over_y().wait_recv()
        self.whole[self.z] = self.mine[...] + self.theirs[...]
        mine = self.whole.at[self.z]
        for d in ORDER_Z:
            self.copy(mine, mine, 2, lax.rem(self.z + d, 8) * 2 + self.y).start()

    def arrive(self):
        self.seven(2).wait_recv()

    def get(self, j):
        return self.whole[:, j].reshape(128, 128)

    def drain(self):
        self.seven(0).wait_send()
        self.over_y().wait_send()
        self.seven(2).wait_send()


class Fold:
    def __init__(self, r, nb, part, yb, half, zb, whole, ss, rs):
        self.r, self.z, self.y = r, r // 2, lax.rem(r, 2)
        self.other = r + 1 - 2 * self.y
        self.nb = nb
        self.part, self.yb, self.half, self.zb, self.whole = part, yb, half, zb, whole
        self.ss, self.rs = ss, rs

    def put(self, j, block):
        self.part[:, :, 8 * j : 8 * j + 8, :] = block.reshape(2, 8, 8, 128)

    def put_rows(self, rows):
        at = 8 * self.nb
        self.part[:, :, at : at + 2, :] = jnp.zeros((2, 8, 2, 128), F32)
        self.part[0, 0, at : at + 2, :] = rows

    def copy(self, src, dst, i, row):
        return pltpu.make_async_remote_copy(
            src_ref=src, dst_ref=dst, send_sem=self.ss.at[i], recv_sem=self.rs.at[i],
            device_id={"row": row}, device_id_type=MESH,
        )

    def over_y(self):
        return self.copy(self.part.at[1 - self.y], self.yb, 0, self.other)

    def seven(self, i):
        return self.copy(self.half.at[pl.ds(1, 7)], self.zb.at[pl.ds(1, 7)], i, self.other)

    def back_y(self):
        mine = self.whole.at[self.y]
        return self.copy(mine, mine, 3, self.other)

    def scatter_y(self):
        self.over_y().start()

    def scatter_z(self):
        self.over_y().wait_recv()
        self.half[...] = self.part[self.y] + self.yb[...]
        for d in ORDER_Z:
            to = lax.rem(self.z + d, 8)
            self.copy(self.half.at[to], self.zb.at[8 - d], 1, to * 2 + self.y).start()

    def gather_z(self):
        self.seven(1).wait_recv()
        total = self.half[self.z]
        for d in range(1, 8):
            total = total + self.zb[d]
        self.whole[self.y, self.z] = total
        mine = self.whole.at[self.y, self.z]
        for d in ORDER_Z:
            self.copy(mine, mine, 2, lax.rem(self.z + d, 8) * 2 + self.y).start()

    def gather_y(self):
        self.seven(2).wait_recv()
        self.back_y().start()

    def arrive(self):
        self.back_y().wait_recv()

    def get(self, j):
        return self.whole[:, :, 8 * j : 8 * j + 8, :].reshape(128, 128)

    def get_row(self, k):
        at = 8 * self.nb + k
        return self.whole[0, 0, at : at + 1, :]

    def drain(self):
        self.over_y().wait_send()
        self.seven(1).wait_send()
        self.seven(2).wait_send()
        self.back_y().wait_send()


ORDER_Z = (4, 3, 5, 2, 6, 1, 7)
def upper():
    r = lax.broadcasted_iota(jnp.int32, (128, 128), 0)
    c = lax.broadcasted_iota(jnp.int32, (128, 128), 1)
    return r < c, r == c


def swap_halves(x):
    return pltpu.roll(x, 64, 1)


def beside(x, y):
    return jnp.where(lax.broadcasted_iota(jnp.int32, x.shape, 1) < 64, x, y)


def norm(block, weight):
    return weight * jnp.sum((block * block).reshape(-1, 8, block.shape[1]), axis=0)


def kernel(x_hbm, mv_ref, nh, zn, *refs):
    n1, n2 = len(CHUNKS1), len(CHUNKS2)
    bufs1, refs = refs[: 5 * n1], refs[5 * n1 :]
    bufs2, refs = refs[: 5 * n2], refs[5 * n2 :]
    (x, xh, xt, a, ah, a2, u, v, z2, z2h, yh, zh, d_out, d_in,
     s_out, s_in, p_out, p_in, q_out, q_in, qt,
     load_sem, ss1, rs1, ss2, rs2, xs, xr) = refs
    r, p = lax.axis_index("row"), lax.axis_index("pair")
    odd = lax.rem(p, 2)
    slow = lax.rem(p + (N - 1) + 2 * odd, N)
    quick = p + 1 - 2 * odd
    first = [
        Fold(r, nb, *bufs1[5 * i : 5 * i + 5], ss1.at[i], rs1.at[i])
        for i, (nb, _) in enumerate(CHUNKS1)
    ]
    second = [
        Line(r, nb, *bufs2[5 * i : 5 * i + 5], ss2.at[i], rs2.at[i])
        for i, nb in enumerate(CHUNKS2)
    ]

    loads = []
    for i, rows in enumerate(tiles(R)):
        c = pltpu.make_async_copy(x_hbm.at[rows], x.at[rows], load_sem.at[i])
        c.start()
        loads.append(c)
    barrier = pltpu.get_barrier_semaphore()
    for d in range(1, N):
        pl.semaphore_signal(
            barrier, inc=1, device_id={"row": lax.rem(r + d, N)}, device_id_type=MESH
        )
    for to in (slow, quick):
        pl.semaphore_signal(barrier, inc=1, device_id={"pair": to}, device_id_type=MESH)

    lead_slow = (mv_ref[...] + odd) == 1
    for i, rows in enumerate(tiles(R)):
        loads[i].wait()
        xl, xr_ = x[rows, :H], x[rows, H:]
        hi, lo = split(jnp.concatenate(
            [jnp.where(lead_slow, xl, xr_), jnp.where(lead_slow, xr_, xl)], axis=1))
        xh[0, rows, :] = hi
        xh[1, rows, :] = lo
        xt[:, rows] = hi.astype(F32).T.astype(BF16)
    sc, qc = pl.ds(0, H), pl.ds(H, H)

    def mixed(i, j):
        return dot(xt[i, :], xh[1, :, j])

    def square(i, j):
        return dot(xt[i, :], xh[0, :, j])

    cross = square(sc, qc) + (mixed(sc, qc) + mixed(qc, sc).T)
    for j in range(4):
        i0, j0 = 128 * (j // 2), 128 * (j % 2)
        first[j // 2].put(j % 2, cross[i0 : i0 + 128, j0 : j0 + 128])
    pl.semaphore_wait(barrier, N + 1)
    first[0].scatter_y()
    first[1].scatter_y()
    above, on = upper()
    packed, diagonal = [], []
    for c, cols in enumerate((sc, qc)):
        m = mixed(cols, cols)
        g = square(cols, cols) + (m + m.T)
        first[2].put(c, g[:128, 128:])
        low = g[128:, 128:]
        first[3].put(c, jnp.where(above | on, g[:128, :128], low))
        diagonal.append(jnp.sum(jnp.where(on, low, 0.0), axis=0, keepdims=True))
    first[3].put_rows(jnp.concatenate(diagonal, axis=0))
    first[2].scatter_y()
    first[3].scatter_y()
    for c in first:
        c.scatter_z()
    for c in first:
        c.gather_z()
    for c in first:
        c.gather_y()

    sq = jnp.zeros((8, 128), F32)
    for j in range(4):
        if j % 2 == 0:
            first[j // 2].arrive()
        i0, j0 = 128 * (j // 2), 128 * (j % 2)
        b = first[j // 2].get(j % 2)
        sq = sq + norm(b, 2.0)
        a[i0 : i0 + 128, H + j0 : H + j0 + 128] = b
        a[H + j0 : H + j0 + 128, i0 : i0 + 128] = b.T
    first[2].arrive()
    for c, o in ((0, 0), (1, H)):
        b = first[2].get(c)
        sq = sq + norm(b, 2.0)
        a[o : o + 128, o + 128 : o + 256] = b
        a[o + 128 : o + 256, o : o + 128] = b.T
    first[3].arrive()
    for c, o in ((0, 0), (1, H)):
        b = first[3].get(c)
        t = b.T
        b0 = jnp.where(above | on, b, t)
        b2 = jnp.where(above, t, jnp.where(on, first[3].get_row(c), b))
        sq = sq + norm(b0, 1.0) + norm(b2, 1.0)
        a[o : o + 128, o : o + 128] = b0
        a[o + 128 : o + 256, o + 128 : o + 256] = b2
    scale = jnp.sqrt(jnp.sum(sq, keepdims=True) + EPS)
    inv = 1.0 / scale
    newton_schulz(a, ah, inv, a2, u, v, z2, z2h, yh)
    back = jnp.sqrt(ROWS / scale)

    def send(src, dst, i, to):
        c = pltpu.make_async_remote_copy(
            src_ref=src, dst_ref=dst, send_sem=xs.at[i], recv_sem=xr.at[i],
            device_id={"pair": to}, device_id_type=MESH,
        )
        c.start()
        return c

    top = 1.5 * z2[sc, :] - 0.5 * product(u, sc, yh)
    left = top[:, H:].T
    hi, lo = split(top[:, :H] * back)
    zh[0, sc, sc], zh[1, sc, sc] = hi, lo
    hi, lo = split(left * back)
    zh[0, qc, sc], zh[1, qc, sc] = hi, lo
    s_sent = []
    rest = []
    for i, rows in enumerate(tiles(R)):
        t = product(xh, rows, zh, sc)
        s_out[rows, :] = t[:, :128]
        s_sent.append(send(s_out.at[rows], s_in.at[rows], i, slow))
        rest.append(t[:, 128:])
    for i, rows in enumerate(tiles(W)):
        p_out[0, rows, :] = beside(rest[i], swap_halves(rest[i + 2]))
        p_out[1, rows, :] = beside(swap_halves(rest[i]), rest[i + 2])
    for c in range(2):
        s_sent.append(send(p_out.at[c], p_in.at[c], 4 + c, slow))
    low = 1.5 * z2[qc, qc] - 0.5 * product(u, qc, yh, qc)
    hi, lo = split(top[:, H:] * back)
    zh[0, sc, qc], zh[1, sc, qc] = hi, lo
    hi, lo = split(low * back)
    zh[0, qc, qc], zh[1, qc, qc] = hi, lo
    for rows in tiles(R):
        q_out[rows, :] = product(xh, rows, zh, qc)
    q_sent = send(q_out, q_in, 6, quick)

    keep(z2h, sc, top)
    keep(z2h, qc, jnp.concatenate([left, low], axis=1))
    for rows, t in zip(tiles(W), symmetric(z2h, ah)):
        keep(v, rows, t * inv)
    d_out[0] = product(z2h, sc, v, sc) * float(ROWS)
    d_out[1] = product(z2h, qc, v, qc) * float(ROWS)
    d_sent = [send(d_out.at[i], d_in.at[i], 7 + i, to) for i, to in ((0, slow), (1, quick))]

    q_sent.wait_recv()
    for rows in tiles(R):
        hi, lo = split(q_in[rows, :])
        nh[0, rows, H:] = hi
        nh[1, rows, H:] = lo
        qt[0, :, rows] = hi.astype(F32).T.astype(BF16)
        qt[1, :, rows] = lo.astype(F32).T.astype(BF16)
    cols = pl.ds(0, 128)
    for i, rows in enumerate(tiles(R)):
        s_sent[i].wait_recv()
        hi, lo = split(s_in[rows, :])
        nh[0, rows, cols] = hi
        nh[1, rows, cols] = lo
    g = dot(qt[0], nh[0, :, cols]) + (dot(qt[0], nh[1, :, cols]) + dot(qt[1], nh[0, :, cols]))
    second[0].put(0, g[:128])
    second[0].put(1, g[128:])
    second[0].scatter()
    for c in range(2):
        s_sent[4 + c].wait_recv()
        hi, lo = split(p_in[c])
        parts = []
        for k in (pl.ds(0, W), pl.ds(W, W)):
            parts.append(dot(qt[0, :, k], hi) + (dot(qt[0, :, k], lo) + dot(qt[1, :, k], hi)))
        g = parts[0] + swap_halves(parts[1])
        second[1 + c].put(0, beside(g[:128], swap_halves(g[128:])))
        second[1 + c].scatter()
    for i, rows in enumerate(tiles(W)):
        p0, p1 = p_in[0, rows, :], p_in[1, rows, :]
        keep(nh, rows, beside(p0, swap_halves(p1)), pl.ds(128, 128))
        keep(nh, pl.ds(W + i * T, T), beside(swap_halves(p0), p1), pl.ds(128, 128))
    second[0].swap()
    second[1].swap()
    second[0].gather()
    second[1].gather()
    second[2].swap()
    second[2].gather()
    for c in d_sent:
        c.wait_recv()
    sq = jnp.zeros((8, 128), F32)
    for i, o in ((0, 0), (1, H)):
        for rows in range(0, H, 128):
            b = d_in[i, rows : rows + 128, :]
            sq = sq + norm(b[:, :128], 1.0) + norm(b[:, 128:], 1.0)
            a[o + rows : o + rows + 128, o : o + H] = b
    def place(j, c, b):
        i0, j0 = H + 128 * j, 128 * c
        a[i0 : i0 + 128, j0 : j0 + 128] = b
        a[j0 : j0 + 128, i0 : i0 + 128] = b.T
        return norm(b, 2.0)

    second[0].arrive()
    for j in range(2):
        sq = sq + place(j, 0, second[0].get(j))
    for c in second[1:]:
        c.arrive()
    b0, b1 = second[1].get(0), second[2].get(0)
    sq = sq + place(0, 1, beside(b0, swap_halves(b1))) + place(1, 1, beside(swap_halves(b0), b1))
    scale = jnp.sqrt(jnp.sum(sq, keepdims=True) + EPS)
    inv = 1.0 / scale
    newton_schulz(a, ah, inv, a2, u, v, z2, z2h, yh)
    back = jnp.sqrt(ROWS / scale)
    top = (1.5 * z2[sc, :] - 0.5 * product(u, sc, yh)) * back
    low = (1.5 * z2[qc, qc] - 0.5 * product(u, qc, yh, qc)) * back
    keep(zn, sc, top)
    keep(zn, qc, jnp.concatenate([top[:, H:].T, low], axis=1))
    for c in s_sent + [q_sent] + d_sent:
        c.wait_send()
    for c in first + second:
        c.drain()


def last(nh, zh, out_hbm, out, out_sem):
    odd = lax.rem(lax.axis_index("pair"), 2)
    s_cols = pl.ds(pl.multiple_of(odd * H, H), H)
    q_cols = pl.ds(pl.multiple_of((1 - odd) * H, H), H)
    stores = []
    for i, rows in enumerate(tiles(R)):
        t = product(nh, rows, zh)
        out[0, rows, :] = t[:, :H]
        out[1, rows, :] = t[:, H:]
        for k, cols in ((0, s_cols), (1, q_cols)):
            c = pltpu.make_async_copy(
                out.at[k, rows], out_hbm.at[rows, cols], out_sem.at[2 * i + k]
            )
            c.start()
            stores.append(c)
    for c in stores:
        c.wait()


def local(slab, moves):
    half = lambda *s: pltpu.VMEM(s, BF16)
    full = lambda *s: pltpu.VMEM(s, F32)
    bufs = []
    for nb, more in CHUNKS1:
        t = (8 * nb + more, 128)
        bufs += [full(2, 8, *t), full(8, *t), full(8, *t), full(8, *t), full(2, 8, *t)]
    for nb in CHUNKS2:
        t = (nb, 16, 128)
        bufs += [full(8, *t), full(8, *t), full(*t), full(*t), full(8, *t)]
    dma = lambda *n: pltpu.SemaphoreType.DMA(n)
    n1, n2 = len(CHUNKS1), len(CHUNKS2)
    vmem = pl.BlockSpec(memory_space=pltpu.VMEM)
    new, root = pl.pallas_call(
        kernel,
        out_shape=[
            jax.ShapeDtypeStruct((2, R, W), BF16),
            jax.ShapeDtypeStruct((2, W, W), BF16),
        ],
        in_specs=[pl.BlockSpec(memory_space=pltpu.HBM), vmem],
        out_specs=[vmem, vmem],
        scratch_shapes=bufs
        + [
            full(R, W), half(2, R, W), half(W, R),
            full(W, W), half(2, W, W), full(W, W), half(2, W, W), half(2, W, W),
            full(W, W), half(2, W, W), half(2, W, W), half(2, W, W),
            full(2, H, H), full(2, H, H),
            full(R, 128), full(R, 128), full(2, W, 128), full(2, W, 128), full(R, H), full(R, H),
            half(2, H, R),
            dma(4), dma(n1, 4), dma(n1, 4), dma(n2, 3), dma(n2, 3), dma(9), dma(9),
        ],
        compiler_params=pltpu.CompilerParams(
            collective_id=1, has_side_effects=True, vmem_limit_bytes=50 * 2**20
        ),
    )(slab, moves)
    return pl.pallas_call(
        last,
        out_shape=jax.ShapeDtypeStruct((R, W), F32),
        in_specs=[vmem, vmem],
        out_specs=pl.BlockSpec(memory_space=pl.ANY),
        scratch_shapes=[full(2, R, H), dma(8)],
        compiler_params=pltpu.CompilerParams(vmem_limit_bytes=16 * 2**20),
    )(new, root)


def solution(mesh):
    placed = (P("row", "pair"), P(None, "pair"))
    return jax.shard_map(
        local, mesh=mesh, in_specs=placed, out_specs=P("row", "pair"), check_vma=False
    )
```

```python
import functools

import jax
import jax.numpy as jnp
from jax import lax
from jax.experimental import pallas as pl
from jax.experimental.pallas import tpu as pltpu
from jax.sharding import PartitionSpec as P

MESH = pl.DeviceIdType.MESH
F32 = jnp.float32
BF16 = jnp.bfloat16
N = 16
H = 256
W = 512
R = 1024
ROWS = 16384
EPS = 1e-06
T = 256
CHUNKS1 = ((2, 0), (2, 0), (2, 2))
LINE1 = 2
CHUNKS2 = (2, 1, 1)


def dot(a, b):
    return jnp.dot(a, b, preferred_element_type=F32)


def split(v):
    hi = v.astype(BF16)
    return hi, (v - hi.astype(F32)).astype(BF16)


def keep(ref, rows, v, cols=slice(None)):
    hi, lo = split(v)
    ref[0, rows, cols] = hi
    ref[1, rows, cols] = lo


def product(a, rows, b, cols=slice(None)):
    ah, al = a[0, rows, :], a[1, rows, :]
    bh, bl = b[0, :, cols], b[1, :, cols]
    return dot(jnp.concatenate([ah, ah, al], axis=1), jnp.concatenate([bl, bh, bh], axis=0))


def tiles(n):
    return [pl.ds(i * T, T) for i in range(n // T)]


def eye_tile(i):
    r = lax.broadcasted_iota(jnp.int32, (T, W), 0) + i * T
    c = lax.broadcasted_iota(jnp.int32, (T, W), 1)
    return jnp.where(r == c, 1.0, 0.0).astype(F32)


def symmetric(a, b):
    top = product(a, pl.ds(0, H), b)
    low = product(a, pl.ds(H, H), b, pl.ds(H, H))
    return top, jnp.concatenate([top[:, H:].T, low], axis=1)


def newton_schulz(a, ah, inv, a2, u, v, z2, z2h, yh):
    for rows in tiles(W):
        keep(ah, rows, a[rows, :])
    inv2 = inv * inv
    for rows, sq in zip(tiles(W), symmetric(ah, ah)):
        at = a[rows, :] * inv
        a[rows, :] = at
        sq = sq * inv2
        a2[rows, :] = sq
        keep(u, rows, sq)
        keep(v, rows, sq - 9.0 * at)
    for i, (rows, p) in enumerate(zip(tiles(W), symmetric(u, v))):
        t = (p + 27.0 * a2[rows, :] - 39.0 * a[rows, :] + 36.0 * eye_tile(i)) * 0.0625
        z2[rows, :] = t
        keep(z2h, rows, t)
    for rows, y in zip(tiles(W), symmetric(z2h, ah)):
        keep(yh, rows, y * inv)
    for rows, t in zip(tiles(W), symmetric(z2h, z2h)):
        keep(u, rows, t)


class Line:
    def __init__(self, r, nb, part, parts, mine, theirs, whole, ss, rs):
        self.r, self.z, self.y = r, r // 2, lax.rem(r, 2)
        self.other = r + 1 - 2 * self.y
        self.part, self.parts, self.mine, self.theirs, self.whole = part, parts, mine, theirs, whole
        self.ss, self.rs = ss, rs

    def put(self, j, block):
        self.part[:, j] = block.reshape(8, 16, 128)

    def copy(self, src, dst, i, row):
        return pltpu.make_async_remote_copy(
            src_ref=src, dst_ref=dst, send_sem=self.ss.at[i], recv_sem=self.rs.at[i],
            device_id={"row": row}, device_id_type=MESH,
        )

    def seven(self, i):
        return self.copy(self.part.at[pl.ds(1, 7)], self.parts.at[pl.ds(1, 7)], i, self.other)

    def over_y(self):
        return self.copy(self.mine, self.theirs, 1, self.other)

    def scatter(self):
        for d in ORDER_Z:
            to = lax.rem(self.z + d, 8)
            self.copy(self.part.at[to], self.parts.at[8 - d], 0, to * 2 + self.y).start()

    def swap(self):
        self.seven(0).wait_recv()
        total = self.part[self.z]
        for d in range(1, 8):
            total = total + self.parts[d]
        self.mine[...] = total
        self.over_y().start()

    def gather(self):
        self.over_y().wait_recv()
        self.whole[self.z] = self.mine[...] + self.theirs[...]
        mine = self.whole.at[self.z]
        for d in ORDER_Z:
            self.copy(mine, mine, 2, lax.rem(self.z + d, 8) * 2 + self.y).start()

    def arrive(self):
        self.seven(2).wait_recv()

    def get(self, j):
        return self.whole[:, j].reshape(128, 128)

    def drain(self):
        self.seven(0).wait_send()
        self.over_y().wait_send()
        self.seven(2).wait_send()


class Fold:
    def __init__(self, r, nb, part, yb, half, zb, whole, ss, rs):
        self.r, self.z, self.y = r, r // 2, lax.rem(r, 2)
        self.other = r + 1 - 2 * self.y
        self.nb = nb
        self.part, self.yb, self.half, self.zb, self.whole = part, yb, half, zb, whole
        self.ss, self.rs = ss, rs

    def put(self, j, block):
        self.part[:, :, 8 * j : 8 * j + 8, :] = block.reshape(2, 8, 8, 128)

    def put_rows(self, rows):
        at = 8 * self.nb
        self.part[:, :, at : at + 2, :] = jnp.zeros((2, 8, 2, 128), F32)
        self.part[0, 0, at : at + 2, :] = rows

    def copy(self, src, dst, i, row):
        return pltpu.make_async_remote_copy(
            src_ref=src, dst_ref=dst, send_sem=self.ss.at[i], recv_sem=self.rs.at[i],
            device_id={"row": row}, device_id_type=MESH,
        )

    def over_y(self):
        return self.copy(self.part.at[1 - self.y], self.yb, 0, self.other)

    def seven(self, i):
        return self.copy(self.half.at[pl.ds(1, 7)], self.zb.at[pl.ds(1, 7)], i, self.other)

    def back_y(self):
        mine = self.whole.at[self.y]
        return self.copy(mine, mine, 3, self.other)

    def scatter_y(self):
        self.over_y().start()

    def scatter_z(self):
        self.over_y().wait_recv()
        self.half[...] = self.part[self.y] + self.yb[...]
        for d in ORDER_Z:
            to = lax.rem(self.z + d, 8)
            self.copy(self.half.at[to], self.zb.at[8 - d], 1, to * 2 + self.y).start()

    def gather_z(self):
        self.seven(1).wait_recv()
        total = self.half[self.z]
        for d in range(1, 8):
            total = total + self.zb[d]
        self.whole[self.y, self.z] = total
        mine = self.whole.at[self.y, self.z]
        for d in ORDER_Z:
            self.copy(mine, mine, 2, lax.rem(self.z + d, 8) * 2 + self.y).start()

    def gather_y(self):
        self.seven(2).wait_recv()
        self.back_y().start()

    def arrive(self):
        self.back_y().wait_recv()

    def get(self, j):
        return self.whole[:, :, 8 * j : 8 * j + 8, :].reshape(128, 128)

    def get_row(self, k):
        at = 8 * self.nb + k
        return self.whole[0, 0, at : at + 1, :]

    def drain(self):
        self.over_y().wait_send()
        self.seven(1).wait_send()
        self.seven(2).wait_send()
        self.back_y().wait_send()


ORDER_Z = (4, 3, 5, 2, 6, 1, 7)
def upper():
    r = lax.broadcasted_iota(jnp.int32, (128, 128), 0)
    c = lax.broadcasted_iota(jnp.int32, (128, 128), 1)
    return r < c, r == c


def swap_halves(x):
    return pltpu.roll(x, 64, 1)


def beside(x, y):
    return jnp.where(lax.broadcasted_iota(jnp.int32, x.shape, 1) < 64, x, y)


def norm(block, weight):
    return weight * jnp.sum((block * block).reshape(-1, 8, block.shape[1]), axis=0)


def kernel(x_hbm, mv_ref, nh, zn, *refs):
    n1, n2 = len(CHUNKS1), 1 + len(CHUNKS2)
    bufs1, refs = refs[: 5 * n1], refs[5 * n1 :]
    bufs2, refs = refs[: 5 * n2], refs[5 * n2 :]
    (x, xh, xt, a, ah, a2, u, v, z2, z2h, yh, zh, d_out, d_in,
     s_out, s_in, p_out, p_in, q_out, q_in, qt,
     load_sem, ss1, rs1, ss2, rs2, xs, xr) = refs
    r, p = lax.axis_index("row"), lax.axis_index("pair")
    odd = lax.rem(p, 2)
    slow = lax.rem(p + (N - 1) + 2 * odd, N)
    quick = p + 1 - 2 * odd
    first = [
        Fold(r, nb, *bufs1[5 * i : 5 * i + 5], ss1.at[i], rs1.at[i])
        for i, (nb, _) in enumerate(CHUNKS1)
    ]
    lines = [
        Line(r, nb, *bufs2[5 * i : 5 * i + 5], ss2.at[i], rs2.at[i])
        for i, nb in enumerate((LINE1, *CHUNKS2))
    ]
    early, second = lines[0], lines[1:]

    loads = []
    for i, rows in enumerate(tiles(R)):
        c = pltpu.make_async_copy(x_hbm.at[rows], x.at[rows], load_sem.at[i])
        c.start()
        loads.append(c)
    barrier = pltpu.get_barrier_semaphore()
    z, y = r // 2, lax.rem(r, 2)
    for row in [lax.rem(z + d, 8) * 2 + y for d in range(1, 8)] + [r + 1 - 2 * y]:
        pl.semaphore_signal(barrier, inc=1, device_id={"row": row}, device_id_type=MESH)
    for to in (slow, quick):
        pl.semaphore_signal(barrier, inc=1, device_id={"pair": to}, device_id_type=MESH)

    lead_slow = (mv_ref[...] + odd) == 1
    for i, rows in enumerate(tiles(R)):
        loads[i].wait()
        xl, xr_ = x[rows, :H], x[rows, H:]
        hi, lo = split(jnp.concatenate(
            [jnp.where(lead_slow, xl, xr_), jnp.where(lead_slow, xr_, xl)], axis=1))
        xh[0, rows, :] = hi
        xh[1, rows, :] = lo
        xt[:, rows] = hi.astype(F32).T.astype(BF16)
    sc, qc = pl.ds(0, H), pl.ds(H, H)

    def mixed(i, j):
        return dot(xt[i, :], xh[1, :, j])

    def square(i, j):
        return dot(xt[i, :], xh[0, :, j])

    left = xt[sc, :]
    cross = mixed(qc, sc).T + dot(
        jnp.concatenate([left, left], axis=1), jnp.concatenate([xh[1, :, qc], xh[0, :, qc]], axis=0)
    )
    for j in range(4):
        i0, j0 = 128 * (j // 2), 128 * (j % 2)
        (early if j < 2 else first[0]).put(j % 2, cross[i0 : i0 + 128, j0 : j0 + 128])
    pl.semaphore_wait(barrier, 10)
    first[0].scatter_y()
    early.scatter()
    above, on = upper()
    packed, diagonal = [], []
    for c, cols in enumerate((sc, qc)):
        m = mixed(cols, cols)
        g = square(cols, cols) + (m + m.T)
        first[1].put(c, g[:128, 128:])
        low = g[128:, 128:]
        first[2].put(c, jnp.where(above | on, g[:128, :128], low))
        diagonal.append(jnp.sum(jnp.where(on, low, 0.0), axis=0, keepdims=True))
    first[2].put_rows(jnp.concatenate(diagonal, axis=0))
    first[1].scatter_y()
    first[2].scatter_y()
    for c in first:
        c.scatter_z()
    early.swap()
    for c in first:
        c.gather_z()
    early.gather()
    for c in first:
        c.gather_y()

    sq = jnp.zeros((8, 128), F32)
    for j in range(4):
        part = early if j < 2 else first[0]
        if j % 2 == 0:
            part.arrive()
        i0, j0 = 128 * (j // 2), 128 * (j % 2)
        b = part.get(j % 2)
        sq = sq + norm(b, 2.0)
        a[i0 : i0 + 128, H + j0 : H + j0 + 128] = b
        a[H + j0 : H + j0 + 128, i0 : i0 + 128] = b.T
    first[1].arrive()
    for c, o in ((0, 0), (1, H)):
        b = first[1].get(c)
        sq = sq + norm(b, 2.0)
        a[o : o + 128, o + 128 : o + 256] = b
        a[o + 128 : o + 256, o : o + 128] = b.T
    first[2].arrive()
    for c, o in ((0, 0), (1, H)):
        b = first[2].get(c)
        t = b.T
        b0 = jnp.where(above | on, b, t)
        b2 = jnp.where(above, t, jnp.where(on, first[2].get_row(c), b))
        sq = sq + norm(b0, 1.0) + norm(b2, 1.0)
        a[o : o + 128, o : o + 128] = b0
        a[o + 128 : o + 256, o + 128 : o + 256] = b2
    scale = jnp.sqrt(jnp.sum(sq, keepdims=True) + EPS)
    inv = 1.0 / scale
    newton_schulz(a, ah, inv, a2, u, v, z2, z2h, yh)
    back = jnp.sqrt(ROWS / scale)

    def send(src, dst, i, to):
        c = pltpu.make_async_remote_copy(
            src_ref=src, dst_ref=dst, send_sem=xs.at[i], recv_sem=xr.at[i],
            device_id={"pair": to}, device_id_type=MESH,
        )
        c.start()
        return c

    top = 1.5 * z2[sc, :] - 0.5 * product(u, sc, yh)
    left = top[:, H:].T
    hi, lo = split(top[:, :H] * back)
    zh[0, sc, sc], zh[1, sc, sc] = hi, lo
    hi, lo = split(left * back)
    zh[0, qc, sc], zh[1, qc, sc] = hi, lo
    s_sent = []
    rest = []
    for i, rows in enumerate(tiles(R)):
        t = product(xh, rows, zh, sc)
        s_out[rows, :] = t[:, :128]
        s_sent.append(send(s_out.at[rows], s_in.at[rows], i, slow))
        rest.append(t[:, 128:])
    for i, rows in enumerate(tiles(W)):
        p_out[0, rows, :] = beside(rest[i], swap_halves(rest[i + 2]))
        p_out[1, rows, :] = beside(swap_halves(rest[i]), rest[i + 2])
    for c in range(2):
        s_sent.append(send(p_out.at[c], p_in.at[c], 4 + c, slow))
    low = 1.5 * z2[qc, qc] - 0.5 * product(u, qc, yh, qc)
    hi, lo = split(top[:, H:] * back)
    zh[0, sc, qc], zh[1, sc, qc] = hi, lo
    hi, lo = split(low * back)
    zh[0, qc, qc], zh[1, qc, qc] = hi, lo
    for rows in tiles(R):
        q_out[rows, :] = product(xh, rows, zh, qc)
    q_sent = send(q_out, q_in, 6, quick)

    keep(z2h, sc, top)
    keep(z2h, qc, jnp.concatenate([left, low], axis=1))
    for rows, t in zip(tiles(W), symmetric(z2h, ah)):
        keep(v, rows, t * inv)
    d_out[0] = product(z2h, sc, v, sc) * float(ROWS)
    d_out[1] = product(z2h, qc, v, qc) * float(ROWS)
    d_sent = [send(d_out.at[i], d_in.at[i], 7 + i, to) for i, to in ((0, slow), (1, quick))]

    q_sent.wait_recv()
    for rows in tiles(R):
        hi, lo = split(q_in[rows, :])
        nh[0, rows, H:] = hi
        nh[1, rows, H:] = lo
        qt[0, :, rows] = hi.astype(F32).T.astype(BF16)
        qt[1, :, rows] = lo.astype(F32).T.astype(BF16)
    cols = pl.ds(0, 128)
    for i, rows in enumerate(tiles(R)):
        s_sent[i].wait_recv()
        hi, lo = split(s_in[rows, :])
        nh[0, rows, cols] = hi
        nh[1, rows, cols] = lo
    g = dot(
        jnp.concatenate([qt[0], qt[0], qt[1]], axis=1),
        jnp.concatenate([nh[1, :, cols], nh[0, :, cols], nh[0, :, cols]], axis=0),
    )
    second[0].put(0, g[:128])
    second[0].put(1, g[128:])
    second[0].scatter()
    for c in range(2):
        s_sent[4 + c].wait_recv()
        hi, lo = split(p_in[c])
        parts = []
        for k in (pl.ds(0, W), pl.ds(W, W)):
            qh = qt[0, :, k]
            parts.append(dot(
                jnp.concatenate([qh, qh, qt[1, :, k]], axis=1), jnp.concatenate([lo, hi, hi], axis=0)
            ))
        g = parts[0] + swap_halves(parts[1])
        second[1 + c].put(0, beside(g[:128], swap_halves(g[128:])))
        second[1 + c].scatter()
    for i, rows in enumerate(tiles(W)):
        p0, p1 = p_in[0, rows, :], p_in[1, rows, :]
        keep(nh, rows, beside(p0, swap_halves(p1)), pl.ds(128, 128))
        keep(nh, pl.ds(W + i * T, T), beside(swap_halves(p0), p1), pl.ds(128, 128))
    second[0].swap()
    second[1].swap()
    second[0].gather()
    second[1].gather()
    second[2].swap()
    second[2].gather()
    for c in d_sent:
        c.wait_recv()
    sq = jnp.zeros((8, 128), F32)
    for i, o in ((0, 0), (1, H)):
        for rows in range(0, H, 128):
            b = d_in[i, rows : rows + 128, :]
            sq = sq + norm(b[:, :128], 1.0) + norm(b[:, 128:], 1.0)
            a[o + rows : o + rows + 128, o : o + H] = b
    def place(j, c, b):
        i0, j0 = H + 128 * j, 128 * c
        a[i0 : i0 + 128, j0 : j0 + 128] = b
        a[j0 : j0 + 128, i0 : i0 + 128] = b.T
        return norm(b, 2.0)

    second[0].arrive()
    for j in range(2):
        sq = sq + place(j, 0, second[0].get(j))
    for c in second[1:]:
        c.arrive()
    b0, b1 = second[1].get(0), second[2].get(0)
    sq = sq + place(0, 1, beside(b0, swap_halves(b1))) + place(1, 1, beside(swap_halves(b0), b1))
    scale = jnp.sqrt(jnp.sum(sq, keepdims=True) + EPS)
    inv = 1.0 / scale
    newton_schulz(a, ah, inv, a2, u, v, z2, z2h, yh)
    back = jnp.sqrt(ROWS / scale)
    top = (1.5 * z2[sc, :] - 0.5 * product(u, sc, yh)) * back
    low = (1.5 * z2[qc, qc] - 0.5 * product(u, qc, yh, qc)) * back
    keep(zn, sc, top)
    keep(zn, qc, jnp.concatenate([top[:, H:].T, low], axis=1))
    for c in s_sent + [q_sent] + d_sent:
        c.wait_send()
    for c in first + lines:
        c.drain()


def last(nh, zh, out_hbm, out, out_sem):
    odd = lax.rem(lax.axis_index("pair"), 2)
    s_cols = pl.ds(pl.multiple_of(odd * H, H), H)
    q_cols = pl.ds(pl.multiple_of((1 - odd) * H, H), H)
    stores = []
    for i in range(2):
        rows = pl.ds(W * i, W)
        t = product(nh, rows, zh)
        out[0, rows, :] = t[:, :H]
        out[1, rows, :] = t[:, H:]
        for k, cols in ((0, s_cols), (1, q_cols)):
            c = pltpu.make_async_copy(
                out.at[k, rows], out_hbm.at[rows, cols], out_sem.at[2 * i + k]
            )
            c.start()
            stores.append(c)
    for c in stores:
        c.wait()


def local(slab, moves):
    half = lambda *s: pltpu.VMEM(s, BF16)
    full = lambda *s: pltpu.VMEM(s, F32)
    bufs = []
    for nb, more in CHUNKS1:
        t = (8 * nb + more, 128)
        bufs += [full(2, 8, *t), full(8, *t), full(8, *t), full(8, *t), full(2, 8, *t)]
    for nb in (LINE1, *CHUNKS2):
        t = (nb, 16, 128)
        bufs += [full(8, *t), full(8, *t), full(*t), full(*t), full(8, *t)]
    dma = lambda *n: pltpu.SemaphoreType.DMA(n)
    n1, n2 = len(CHUNKS1), 1 + len(CHUNKS2)
    vmem = pl.BlockSpec(memory_space=pltpu.VMEM)
    new, root = pl.pallas_call(
        kernel,
        out_shape=[
            jax.ShapeDtypeStruct((2, R, W), BF16),
            jax.ShapeDtypeStruct((2, W, W), BF16),
        ],
        in_specs=[pl.BlockSpec(memory_space=pltpu.HBM), vmem],
        out_specs=[vmem, vmem],
        scratch_shapes=bufs
        + [
            full(R, W), half(2, R, W), half(W, R),
            full(W, W), half(2, W, W), full(W, W), half(2, W, W), half(2, W, W),
            full(W, W), half(2, W, W), half(2, W, W), half(2, W, W),
            full(2, H, H), full(2, H, H),
            full(R, 128), full(R, 128), full(2, W, 128), full(2, W, 128), full(R, H), full(R, H),
            half(2, H, R),
            dma(4), dma(n1, 4), dma(n1, 4), dma(n2, 3), dma(n2, 3), dma(9), dma(9),
        ],
        compiler_params=pltpu.CompilerParams(
            collective_id=1, has_side_effects=True, vmem_limit_bytes=50 * 2**20
        ),
    )(slab, moves)
    return pl.pallas_call(
        last,
        out_shape=jax.ShapeDtypeStruct((R, W), F32),
        in_specs=[vmem, vmem],
        out_specs=pl.BlockSpec(memory_space=pl.ANY),
        scratch_shapes=[full(2, R, H), dma(8)],
        compiler_params=pltpu.CompilerParams(vmem_limit_bytes=16 * 2**20),
    )(new, root)


def solution(mesh):
    placed = (P("row", "pair"), P(None, "pair"))
    return jax.shard_map(
        local, mesh=mesh, in_specs=placed, out_specs=P("row", "pair"), check_vma=False
    )
```

```python
import functools

import jax
import jax.numpy as jnp
from jax import lax
from jax.experimental import pallas as pl
from jax.experimental.pallas import tpu as pltpu
from jax.sharding import PartitionSpec as P

MESH = pl.DeviceIdType.MESH
F32 = jnp.float32
BF16 = jnp.bfloat16
N = 16
H = 256
W = 512
R = 1024
ROWS = 16384
EPS = 1e-06
T = 256
CHUNKS1 = ((2, 0), (2, 0), (1, 2), (1, 2))
LINE1 = 2
CHUNKS2 = (2, 1, 1)


def dot(a, b):
    return jnp.dot(a, b, preferred_element_type=F32)


def split(v):
    hi = v.astype(BF16)
    return hi, (v - hi.astype(F32)).astype(BF16)


def keep(ref, rows, v, cols=slice(None)):
    hi, lo = split(v)
    ref[0, rows, cols] = hi
    ref[1, rows, cols] = lo


def product(a, rows, b, cols=slice(None)):
    ah, al = a[0, rows, :], a[1, rows, :]
    bh, bl = b[0, :, cols], b[1, :, cols]
    return dot(jnp.concatenate([ah, ah, al], axis=1), jnp.concatenate([bl, bh, bh], axis=0))


def tiles(n):
    return [pl.ds(i * T, T) for i in range(n // T)]


def eye_tile(i):
    r = lax.broadcasted_iota(jnp.int32, (T, W), 0) + i * T
    c = lax.broadcasted_iota(jnp.int32, (T, W), 1)
    return jnp.where(r == c, 1.0, 0.0).astype(F32)


def symmetric(a, b):
    top = product(a, pl.ds(0, H), b)
    low = product(a, pl.ds(H, H), b, pl.ds(H, H))
    return top, jnp.concatenate([top[:, H:].T, low], axis=1)


def newton_schulz(a, ah, inv, a2, u, v, z2, z2h, yh):
    inv2 = inv * inv
    for rows, sq in zip(tiles(W), symmetric(ah, ah)):
        at = a[rows, :] * inv
        a[rows, :] = at
        sq = sq * inv2
        a2[rows, :] = sq
        keep(u, rows, sq)
        keep(v, rows, sq - 9.0 * at)
    for i, (rows, p) in enumerate(zip(tiles(W), symmetric(u, v))):
        t = (p + 27.0 * a2[rows, :] - 39.0 * a[rows, :] + 36.0 * eye_tile(i)) * 0.0625
        z2[rows, :] = t
        keep(z2h, rows, t)
    for rows, y in zip(tiles(W), symmetric(z2h, ah)):
        keep(yh, rows, y * inv)
    for rows, t in zip(tiles(W), symmetric(z2h, z2h)):
        keep(u, rows, t)


class Line:
    def __init__(self, r, nb, part, parts, mine, theirs, whole, ss, rs):
        self.r, self.z, self.y = r, r // 2, lax.rem(r, 2)
        self.other = r + 1 - 2 * self.y
        self.part, self.parts, self.mine, self.theirs, self.whole = part, parts, mine, theirs, whole
        self.ss, self.rs = ss, rs

    def put(self, j, block):
        self.part[:, j] = block.reshape(8, 16, 128)

    def copy(self, src, dst, i, row):
        return pltpu.make_async_remote_copy(
            src_ref=src, dst_ref=dst, send_sem=self.ss.at[i], recv_sem=self.rs.at[i],
            device_id={"row": row}, device_id_type=MESH,
        )

    def seven(self, i):
        return self.copy(self.part.at[pl.ds(1, 7)], self.parts.at[pl.ds(1, 7)], i, self.other)

    def over_y(self):
        return self.copy(self.mine, self.theirs, 1, self.other)

    def scatter(self):
        for d in ORDER_Z:
            to = lax.rem(self.z + d, 8)
            self.copy(self.part.at[to], self.parts.at[8 - d], 0, to * 2 + self.y).start()

    def swap(self):
        self.seven(0).wait_recv()
        total = self.part[self.z]
        for d in range(1, 8):
            total = total + self.parts[d]
        self.mine[...] = total
        self.over_y().start()

    def gather(self):
        self.over_y().wait_recv()
        self.whole[self.z] = self.mine[...] + self.theirs[...]
        mine = self.whole.at[self.z]
        for d in ORDER_Z:
            self.copy(mine, mine, 2, lax.rem(self.z + d, 8) * 2 + self.y).start()

    def arrive(self):
        self.seven(2).wait_recv()

    def get(self, j):
        return self.whole[:, j].reshape(128, 128)

    def drain(self):
        self.seven(0).wait_send()
        self.over_y().wait_send()
        self.seven(2).wait_send()


class Fold:
    def __init__(self, r, nb, part, yb, half, zb, whole, ss, rs):
        self.r, self.z, self.y = r, r // 2, lax.rem(r, 2)
        self.other = r + 1 - 2 * self.y
        self.nb = nb
        self.part, self.yb, self.half, self.zb, self.whole = part, yb, half, zb, whole
        self.ss, self.rs = ss, rs

    def put(self, j, block):
        self.part[:, :, 8 * j : 8 * j + 8, :] = block.reshape(2, 8, 8, 128)

    def put_rows(self, rows):
        at = 8 * self.nb
        self.part[:, :, at : at + 2, :] = jnp.zeros((2, 8, 2, 128), F32)
        self.part[0, 0, at : at + 2, :] = rows

    def copy(self, src, dst, i, row):
        return pltpu.make_async_remote_copy(
            src_ref=src, dst_ref=dst, send_sem=self.ss.at[i], recv_sem=self.rs.at[i],
            device_id={"row": row}, device_id_type=MESH,
        )

    def over_y(self):
        return self.copy(self.part.at[1 - self.y], self.yb, 0, self.other)

    def seven(self, i):
        return self.copy(self.half.at[pl.ds(1, 7)], self.zb.at[pl.ds(1, 7)], i, self.other)

    def back_y(self):
        mine = self.whole.at[self.y]
        return self.copy(mine, mine, 3, self.other)

    def scatter_y(self):
        self.over_y().start()

    def scatter_z(self):
        self.over_y().wait_recv()
        self.half[...] = self.part[self.y] + self.yb[...]
        for d in ORDER_Z:
            to = lax.rem(self.z + d, 8)
            self.copy(self.half.at[to], self.zb.at[8 - d], 1, to * 2 + self.y).start()

    def gather_z(self):
        self.seven(1).wait_recv()
        total = self.half[self.z]
        for d in range(1, 8):
            total = total + self.zb[d]
        self.whole[self.y, self.z] = total
        mine = self.whole.at[self.y, self.z]
        for d in ORDER_Z:
            self.copy(mine, mine, 2, lax.rem(self.z + d, 8) * 2 + self.y).start()

    def gather_y(self):
        self.seven(2).wait_recv()
        self.back_y().start()

    def arrive(self):
        self.back_y().wait_recv()

    def get(self, j):
        return self.whole[:, :, 8 * j : 8 * j + 8, :].reshape(128, 128)

    def get_row(self, k):
        at = 8 * self.nb + k
        return self.whole[0, 0, at : at + 1, :]

    def drain(self):
        self.over_y().wait_send()
        self.seven(1).wait_send()
        self.seven(2).wait_send()
        self.back_y().wait_send()


ORDER_Z = (4, 3, 5, 2, 6, 1, 7)
def upper():
    r = lax.broadcasted_iota(jnp.int32, (128, 128), 0)
    c = lax.broadcasted_iota(jnp.int32, (128, 128), 1)
    return r < c, r == c


def swap_halves(x):
    return pltpu.roll(x, 64, 1)


def beside(x, y):
    return jnp.where(lax.broadcasted_iota(jnp.int32, x.shape, 1) < 64, x, y)


def norm(block, weight):
    return weight * jnp.sum((block * block).reshape(-1, 8, block.shape[1]), axis=0)


def kernel(x_hbm, mv_ref, nh, zn, *refs):
    n1, n2 = len(CHUNKS1), 1 + len(CHUNKS2)
    bufs1, refs = refs[: 5 * n1], refs[5 * n1 :]
    bufs2, refs = refs[: 5 * n2], refs[5 * n2 :]
    (x, xh, xt, a, ah, a2, u, v, z2, z2h, yh, zh, d_out, d_in,
     s_out, s_in, p_out, p_in, q_out, q_in, qt,
     load_sem, ss1, rs1, ss2, rs2, xs, xr) = refs
    r, p = lax.axis_index("row"), lax.axis_index("pair")
    odd = lax.rem(p, 2)
    slow = lax.rem(p + (N - 1) + 2 * odd, N)
    quick = p + 1 - 2 * odd
    first = [
        Fold(r, nb, *bufs1[5 * i : 5 * i + 5], ss1.at[i], rs1.at[i])
        for i, (nb, _) in enumerate(CHUNKS1)
    ]
    lines = [
        Line(r, nb, *bufs2[5 * i : 5 * i + 5], ss2.at[i], rs2.at[i])
        for i, nb in enumerate((LINE1, *CHUNKS2))
    ]
    early, second = lines[0], lines[1:]

    loads = []
    for i, rows in enumerate(tiles(R)):
        c = pltpu.make_async_copy(x_hbm.at[rows], x.at[rows], load_sem.at[i])
        c.start()
        loads.append(c)
    barrier = pltpu.get_barrier_semaphore()
    z, y = r // 2, lax.rem(r, 2)
    for row in [lax.rem(z + d, 8) * 2 + y for d in range(1, 8)] + [r + 1 - 2 * y]:
        pl.semaphore_signal(barrier, inc=1, device_id={"row": row}, device_id_type=MESH)
    for to in (slow, quick):
        pl.semaphore_signal(barrier, inc=1, device_id={"pair": to}, device_id_type=MESH)

    lead_slow = (mv_ref[...] + odd) == 1
    for i, rows in enumerate(tiles(R)):
        loads[i].wait()
        xl, xr_ = x[rows, :H], x[rows, H:]
        hi, lo = split(jnp.concatenate(
            [jnp.where(lead_slow, xl, xr_), jnp.where(lead_slow, xr_, xl)], axis=1))
        xh[0, rows, :] = hi
        xh[1, rows, :] = lo
        xt[:, rows] = hi.astype(F32).T.astype(BF16)
    sc, qc = pl.ds(0, H), pl.ds(H, H)

    def mixed(i, j):
        return dot(xt[i, :], xh[1, :, j])

    def square(i, j):
        return dot(xt[i, :], xh[0, :, j])

    left = xt[sc, :]
    cross = mixed(qc, sc).T + dot(
        jnp.concatenate([left, left], axis=1), jnp.concatenate([xh[1, :, qc], xh[0, :, qc]], axis=0)
    )
    for j in range(4):
        i0, j0 = 128 * (j // 2), 128 * (j % 2)
        (early if j < 2 else first[0]).put(j % 2, cross[i0 : i0 + 128, j0 : j0 + 128])
    pl.semaphore_wait(barrier, 10)
    first[0].scatter_y()
    early.scatter()
    above, on = upper()
    for c, cols in enumerate((sc, qc)):
        m = mixed(cols, cols)
        g = square(cols, cols) + (m + m.T)
        first[1].put(c, g[:128, 128:])
        low = g[128:, 128:]
        last_of = first[2 + c]
        last_of.put(0, jnp.where(above | on, g[:128, :128], low))
        diagonal = jnp.sum(jnp.where(on, low, 0.0), axis=0, keepdims=True)
        last_of.put_rows(jnp.concatenate([diagonal, diagonal], axis=0))
    for c in first[1:]:
        c.scatter_y()
    for c in first:
        c.scatter_z()
    early.swap()
    for c in first:
        c.gather_z()
    early.gather()
    for c in first:
        c.gather_y()

    def place(i0, j0, b):
        a[i0 : i0 + b.shape[0], j0 : j0 + b.shape[1]] = b
        keep(ah, slice(i0, i0 + b.shape[0]), b, slice(j0, j0 + b.shape[1]))

    def place_both(i0, j0, b):
        place(i0, j0, b)
        place(j0, i0, b.T)
        return norm(b, 2.0)

    sq = jnp.zeros((8, 128), F32)
    for j in range(4):
        part = early if j < 2 else first[0]
        if j % 2 == 0:
            part.arrive()
        sq = sq + place_both(128 * (j // 2), H + 128 * (j % 2), part.get(j % 2))
    first[1].arrive()
    for c, o in ((0, 0), (1, H)):
        sq = sq + place_both(o, o + 128, first[1].get(c))
    for c, o in ((0, 0), (1, H)):
        first[2 + c].arrive()
        b = first[2 + c].get(0)
        t = b.T
        b0 = jnp.where(above | on, b, t)
        b2 = jnp.where(above, t, jnp.where(on, first[2 + c].get_row(0), b))
        sq = sq + norm(b0, 1.0) + norm(b2, 1.0)
        place(o, o, b0)
        place(o + 128, o + 128, b2)
    scale = jnp.sqrt(jnp.sum(sq, keepdims=True) + EPS)
    inv = 1.0 / scale
    newton_schulz(a, ah, inv, a2, u, v, z2, z2h, yh)
    back = jnp.sqrt(ROWS / scale)

    def send(src, dst, i, to):
        c = pltpu.make_async_remote_copy(
            src_ref=src, dst_ref=dst, send_sem=xs.at[i], recv_sem=xr.at[i],
            device_id={"pair": to}, device_id_type=MESH,
        )
        c.start()
        return c

    top = 1.5 * z2[sc, :] - 0.5 * product(u, sc, yh)
    left = top[:, H:].T
    hi, lo = split(top[:, :H] * back)
    zh[0, sc, sc], zh[1, sc, sc] = hi, lo
    hi, lo = split(left * back)
    zh[0, qc, sc], zh[1, qc, sc] = hi, lo
    s_sent = []
    rest = []
    for i, rows in enumerate(tiles(R)):
        t = product(xh, rows, zh, sc)
        s_out[rows, :] = t[:, :128]
        s_sent.append(send(s_out.at[rows], s_in.at[rows], i, slow))
        rest.append(t[:, 128:])
    for i, rows in enumerate(tiles(W)):
        p_out[0, rows, :] = beside(rest[i], swap_halves(rest[i + 2]))
        p_out[1, rows, :] = beside(swap_halves(rest[i]), rest[i + 2])
    for c in range(2):
        s_sent.append(send(p_out.at[c], p_in.at[c], 4 + c, slow))
    low = 1.5 * z2[qc, qc] - 0.5 * product(u, qc, yh, qc)
    hi, lo = split(top[:, H:] * back)
    zh[0, sc, qc], zh[1, sc, qc] = hi, lo
    hi, lo = split(low * back)
    zh[0, qc, qc], zh[1, qc, qc] = hi, lo
    for rows in tiles(R):
        q_out[rows, :] = product(xh, rows, zh, qc)
    q_sent = send(q_out, q_in, 6, quick)

    keep(z2h, sc, top)
    keep(z2h, qc, jnp.concatenate([left, low], axis=1))
    for rows, t in zip(tiles(W), symmetric(z2h, ah)):
        keep(v, rows, t * inv)
    d_out[0] = product(z2h, sc, v, sc) * float(ROWS)
    d_out[1] = product(z2h, qc, v, qc) * float(ROWS)
    d_sent = [send(d_out.at[i], d_in.at[i], 7 + i, to) for i, to in ((0, slow), (1, quick))]

    q_sent.wait_recv()
    for rows in tiles(R):
        hi, lo = split(q_in[rows, :])
        nh[0, rows, H:] = hi
        nh[1, rows, H:] = lo
        qt[0, :, rows] = hi.astype(F32).T.astype(BF16)
        qt[1, :, rows] = lo.astype(F32).T.astype(BF16)
    cols = pl.ds(0, 128)
    for i, rows in enumerate(tiles(R)):
        s_sent[i].wait_recv()
        hi, lo = split(s_in[rows, :])
        nh[0, rows, cols] = hi
        nh[1, rows, cols] = lo
    g = dot(
        jnp.concatenate([qt[0], qt[0], qt[1]], axis=1),
        jnp.concatenate([nh[1, :, cols], nh[0, :, cols], nh[0, :, cols]], axis=0),
    )
    second[0].put(0, g[:128])
    second[0].put(1, g[128:])
    second[0].scatter()
    for c in range(2):
        s_sent[4 + c].wait_recv()
        hi, lo = split(p_in[c])
        parts = []
        for k in (pl.ds(0, W), pl.ds(W, W)):
            qh = qt[0, :, k]
            parts.append(dot(
                jnp.concatenate([qh, qh, qt[1, :, k]], axis=1), jnp.concatenate([lo, hi, hi], axis=0)
            ))
        g = parts[0] + swap_halves(parts[1])
        second[1 + c].put(0, beside(g[:128], swap_halves(g[128:])))
        second[1 + c].scatter()
    for i, rows in enumerate(tiles(W)):
        p0, p1 = p_in[0, rows, :], p_in[1, rows, :]
        keep(nh, rows, beside(p0, swap_halves(p1)), pl.ds(128, 128))
        keep(nh, pl.ds(W + i * T, T), beside(swap_halves(p0), p1), pl.ds(128, 128))
    second[0].swap()
    second[1].swap()
    second[0].gather()
    second[1].gather()
    second[2].swap()
    second[2].gather()
    for c in d_sent:
        c.wait_recv()
    sq = jnp.zeros((8, 128), F32)
    for i, o in ((0, 0), (1, H)):
        b = d_in[i]
        sq = sq + norm(b[:, :128], 1.0) + norm(b[:, 128:], 1.0)
        place(o, o, b)
    second[0].arrive()
    for j in range(2):
        sq = sq + place_both(H + 128 * j, 0, second[0].get(j))
    for c in second[1:]:
        c.arrive()
    b0, b1 = second[1].get(0), second[2].get(0)
    sq = sq + place_both(H, 128, beside(b0, swap_halves(b1)))
    sq = sq + place_both(H + 128, 128, beside(swap_halves(b0), b1))
    scale = jnp.sqrt(jnp.sum(sq, keepdims=True) + EPS)
    inv = 1.0 / scale
    newton_schulz(a, ah, inv, a2, u, v, z2, z2h, yh)
    back = jnp.sqrt(ROWS / scale)
    top = (1.5 * z2[sc, :] - 0.5 * product(u, sc, yh)) * back
    low = (1.5 * z2[qc, qc] - 0.5 * product(u, qc, yh, qc)) * back
    keep(zn, sc, top)
    keep(zn, qc, jnp.concatenate([top[:, H:].T, low], axis=1))
    for c in s_sent + [q_sent] + d_sent:
        c.wait_send()
    for c in first + lines:
        c.drain()


def last(nh, zh, out_hbm, out, out_sem):
    odd = lax.rem(lax.axis_index("pair"), 2)
    s_cols = pl.ds(pl.multiple_of(odd * H, H), H)
    q_cols = pl.ds(pl.multiple_of((1 - odd) * H, H), H)
    stores = []
    for i in range(2):
        rows = pl.ds(W * i, W)
        t = product(nh, rows, zh)
        out[0, rows, :] = t[:, :H]
        out[1, rows, :] = t[:, H:]
        for k, cols in ((0, s_cols), (1, q_cols)):
            c = pltpu.make_async_copy(
                out.at[k, rows], out_hbm.at[rows, cols], out_sem.at[2 * i + k]
            )
            c.start()
            stores.append(c)
    for c in stores:
        c.wait()


def local(slab, moves):
    half = lambda *s: pltpu.VMEM(s, BF16)
    full = lambda *s: pltpu.VMEM(s, F32)
    bufs = []
    for nb, more in CHUNKS1:
        t = (8 * nb + more, 128)
        bufs += [full(2, 8, *t), full(8, *t), full(8, *t), full(8, *t), full(2, 8, *t)]
    for nb in (LINE1, *CHUNKS2):
        t = (nb, 16, 128)
        bufs += [full(8, *t), full(8, *t), full(*t), full(*t), full(8, *t)]
    dma = lambda *n: pltpu.SemaphoreType.DMA(n)
    n1, n2 = len(CHUNKS1), 1 + len(CHUNKS2)
    vmem = pl.BlockSpec(memory_space=pltpu.VMEM)
    new, root = pl.pallas_call(
        kernel,
        out_shape=[
            jax.ShapeDtypeStruct((2, R, W), BF16),
            jax.ShapeDtypeStruct((2, W, W), BF16),
        ],
        in_specs=[pl.BlockSpec(memory_space=pltpu.HBM), vmem],
        out_specs=[vmem, vmem],
        scratch_shapes=bufs
        + [
            full(R, W), half(2, R, W), half(W, R),
            full(W, W), half(2, W, W), full(W, W), half(2, W, W), half(2, W, W),
            full(W, W), half(2, W, W), half(2, W, W), half(2, W, W),
            full(2, H, H), full(2, H, H),
            full(R, 128), full(R, 128), full(2, W, 128), full(2, W, 128), full(R, H), full(R, H),
            half(2, H, R),
            dma(4), dma(n1, 4), dma(n1, 4), dma(n2, 3), dma(n2, 3), dma(9), dma(9),
        ],
        compiler_params=pltpu.CompilerParams(
            collective_id=1, has_side_effects=True, vmem_limit_bytes=50 * 2**20
        ),
    )(slab, moves)
    return pl.pallas_call(
        last,
        out_shape=jax.ShapeDtypeStruct((R, W), F32),
        in_specs=[vmem, vmem],
        out_specs=pl.BlockSpec(memory_space=pl.ANY),
        scratch_shapes=[full(2, R, H), dma(8)],
        compiler_params=pltpu.CompilerParams(vmem_limit_bytes=16 * 2**20),
    )(new, root)


def solution(mesh):
    placed = (P("row", "pair"), P(None, "pair"))
    return jax.shard_map(
        local, mesh=mesh, in_specs=placed, out_specs=P("row", "pair"), check_vma=False
    )
```

```python
import functools

import jax
import jax.numpy as jnp
from jax import lax
from jax.experimental import pallas as pl
from jax.experimental.pallas import tpu as pltpu
from jax.sharding import PartitionSpec as P

MESH = pl.DeviceIdType.MESH
F32 = jnp.float32
BF16 = jnp.bfloat16
N = 16
H = 256
W = 512
R = 1024
ROWS = 16384
EPS = 1e-06
T = 256
CHUNKS1 = ((2, 0), (2, 0), (2, 2))
LINE1 = 2
CHUNKS2 = (2, 1, 1)


def dot(a, b):
    return jnp.dot(a, b, preferred_element_type=F32)


def split(v):
    hi = v.astype(BF16)
    return hi, (v - hi.astype(F32)).astype(BF16)


def keep(ref, rows, v, cols=slice(None)):
    hi, lo = split(v)
    ref[0, rows, cols] = hi
    ref[1, rows, cols] = lo


def product(a, rows, b, cols=slice(None)):
    ah, al = a[0, rows, :], a[1, rows, :]
    bh, bl = b[0, :, cols], b[1, :, cols]
    return dot(jnp.concatenate([ah, ah, al], axis=1), jnp.concatenate([bl, bh, bh], axis=0))


def tiles(n):
    return [pl.ds(i * T, T) for i in range(n // T)]


def eye_tile(i):
    r = lax.broadcasted_iota(jnp.int32, (T, W), 0) + i * T
    c = lax.broadcasted_iota(jnp.int32, (T, W), 1)
    return jnp.where(r == c, 1.0, 0.0).astype(F32)


def symmetric(a, b):
    top = product(a, pl.ds(0, H), b)
    low = product(a, pl.ds(H, H), b, pl.ds(H, H))
    return top, jnp.concatenate([top[:, H:].T, low], axis=1)


def newton_schulz(a, ah, inv, a2, u, v, z2, z2h, yh):
    for rows in tiles(W):
        keep(ah, rows, a[rows, :])
    inv2 = inv * inv
    for rows, sq in zip(tiles(W), symmetric(ah, ah)):
        at = a[rows, :] * inv
        a[rows, :] = at
        sq = sq * inv2
        a2[rows, :] = sq
        keep(u, rows, sq)
        keep(v, rows, sq - 9.0 * at)
    for i, (rows, p) in enumerate(zip(tiles(W), symmetric(u, v))):
        t = (p + 27.0 * a2[rows, :] - 39.0 * a[rows, :] + 36.0 * eye_tile(i)) * 0.0625
        z2[rows, :] = t
        keep(z2h, rows, t)
    for rows, y in zip(tiles(W), symmetric(z2h, ah)):
        keep(yh, rows, y * inv)
    for rows, t in zip(tiles(W), symmetric(z2h, z2h)):
        keep(u, rows, t)


class Line:
    def __init__(self, r, nb, part, parts, mine, theirs, whole, ss, rs):
        self.r, self.z, self.y = r, r // 2, lax.rem(r, 2)
        self.other = r + 1 - 2 * self.y
        self.part, self.parts, self.mine, self.theirs, self.whole = part, parts, mine, theirs, whole
        self.ss, self.rs = ss, rs

    def put(self, j, block):
        self.part[:, j] = block.reshape(8, 16, 128)

    def copy(self, src, dst, i, row):
        return pltpu.make_async_remote_copy(
            src_ref=src, dst_ref=dst, send_sem=self.ss.at[i], recv_sem=self.rs.at[i],
            device_id={"row": row}, device_id_type=MESH,
        )

    def seven(self, i):
        return self.copy(self.part.at[pl.ds(1, 7)], self.parts.at[pl.ds(1, 7)], i, self.other)

    def over_y(self):
        return self.copy(self.mine, self.theirs, 1, self.other)

    def scatter(self):
        for d in ORDER_Z:
            to = lax.rem(self.z + d, 8)
            self.copy(self.part.at[to], self.parts.at[8 - d], 0, to * 2 + self.y).start()

    def swap(self):
        self.seven(0).wait_recv()
        total = self.part[self.z]
        for d in range(1, 8):
            total = total + self.parts[d]
        self.mine[...] = total
        self.over_y().start()

    def gather(self):
        self.over_y().wait_recv()
        self.whole[self.z] = self.mine[...] + self.theirs[...]
        mine = self.whole.at[self.z]
        for d in ORDER_Z:
            self.copy(mine, mine, 2, lax.rem(self.z + d, 8) * 2 + self.y).start()

    def arrive(self):
        self.seven(2).wait_recv()

    def get(self, j):
        return self.whole[:, j].reshape(128, 128)

    def drain(self):
        self.seven(0).wait_send()
        self.over_y().wait_send()
        self.seven(2).wait_send()


class Fold:
    def __init__(self, r, nb, part, yb, half, zb, whole, ss, rs):
        self.r, self.z, self.y = r, r // 2, lax.rem(r, 2)
        self.other = r + 1 - 2 * self.y
        self.nb = nb
        self.part, self.yb, self.half, self.zb, self.whole = part, yb, half, zb, whole
        self.ss, self.rs = ss, rs

    def put(self, j, block):
        self.part[:, :, 8 * j : 8 * j + 8, :] = block.reshape(2, 8, 8, 128)

    def put_rows(self, rows):
        at = 8 * self.nb
        self.part[:, :, at : at + 2, :] = jnp.zeros((2, 8, 2, 128), F32)
        self.part[0, 0, at : at + 2, :] = rows

    def copy(self, src, dst, i, row):
        return pltpu.make_async_remote_copy(
            src_ref=src, dst_ref=dst, send_sem=self.ss.at[i], recv_sem=self.rs.at[i],
            device_id={"row": row}, device_id_type=MESH,
        )

    def over_y(self):
        return self.copy(self.part.at[1 - self.y], self.yb, 0, self.other)

    def seven(self, i):
        return self.copy(self.half.at[pl.ds(1, 7)], self.zb.at[pl.ds(1, 7)], i, self.other)

    def back_y(self):
        mine = self.whole.at[self.y]
        return self.copy(mine, mine, 3, self.other)

    def scatter_y(self):
        self.over_y().start()

    def scatter_z(self):
        self.over_y().wait_recv()
        self.half[...] = self.part[self.y] + self.yb[...]
        for d in ORDER_Z:
            to = lax.rem(self.z + d, 8)
            self.copy(self.half.at[to], self.zb.at[8 - d], 1, to * 2 + self.y).start()

    def gather_z(self):
        self.seven(1).wait_recv()
        total = self.half[self.z]
        for d in range(1, 8):
            total = total + self.zb[d]
        self.whole[self.y, self.z] = total
        mine = self.whole.at[self.y, self.z]
        for d in ORDER_Z:
            self.copy(mine, mine, 2, lax.rem(self.z + d, 8) * 2 + self.y).start()

    def gather_y(self):
        self.seven(2).wait_recv()
        self.back_y().start()

    def arrive(self):
        self.back_y().wait_recv()

    def get(self, j):
        return self.whole[:, :, 8 * j : 8 * j + 8, :].reshape(128, 128)

    def get_row(self, k):
        at = 8 * self.nb + k
        return self.whole[0, 0, at : at + 1, :]

    def drain(self):
        self.over_y().wait_send()
        self.seven(1).wait_send()
        self.seven(2).wait_send()
        self.back_y().wait_send()


ORDER_Z = (4, 3, 5, 2, 6, 1, 7)
def upper():
    r = lax.broadcasted_iota(jnp.int32, (128, 128), 0)
    c = lax.broadcasted_iota(jnp.int32, (128, 128), 1)
    return r < c, r == c


def swap_halves(x):
    return pltpu.roll(x, 64, 1)


def beside(x, y):
    return jnp.where(lax.broadcasted_iota(jnp.int32, x.shape, 1) < 64, x, y)


def norm(block, weight):
    return weight * jnp.sum((block * block).reshape(-1, 8, block.shape[1]), axis=0)


def kernel(x_hbm, mv_ref, nh, zn, *refs):
    n1, n2 = len(CHUNKS1), 1 + len(CHUNKS2)
    bufs1, refs = refs[: 5 * n1], refs[5 * n1 :]
    bufs2, refs = refs[: 5 * n2], refs[5 * n2 :]
    (x, xh, xt, a, ah, a2, u, v, z2, z2h, yh, zh, d_out, d_in,
     s_out, s_in, p_out, p_in, q_out, q_in, qt,
     load_sem, ss1, rs1, ss2, rs2, xs, xr) = refs
    r, p = lax.axis_index("row"), lax.axis_index("pair")
    odd = lax.rem(p, 2)
    slow = lax.rem(p + (N - 1) + 2 * odd, N)
    quick = p + 1 - 2 * odd
    first = [
        Fold(r, nb, *bufs1[5 * i : 5 * i + 5], ss1.at[i], rs1.at[i])
        for i, (nb, _) in enumerate(CHUNKS1)
    ]
    lines = [
        Line(r, nb, *bufs2[5 * i : 5 * i + 5], ss2.at[i], rs2.at[i])
        for i, nb in enumerate((LINE1, *CHUNKS2))
    ]
    early, second = lines[0], lines[1:]

    barrier = pltpu.get_barrier_semaphore()
    z, y = r // 2, lax.rem(r, 2)
    for row in [lax.rem(z + d, 8) * 2 + y for d in ORDER_Z] + [r + 1 - 2 * y]:
        pl.semaphore_signal(barrier, inc=1, device_id={"row": row}, device_id_type=MESH)
    for to in (slow, quick):
        pl.semaphore_signal(barrier, inc=1, device_id={"pair": to}, device_id_type=MESH)
    loads = []
    for i, rows in enumerate(tiles(R)):
        c = pltpu.make_async_copy(x_hbm.at[rows], x.at[rows], load_sem.at[i])
        c.start()
        loads.append(c)

    lead_slow = (mv_ref[...] + odd) == 1
    for i, rows in enumerate(tiles(R)):
        loads[i].wait()
        xl, xr_ = x[rows, :H], x[rows, H:]
        hi, lo = split(jnp.concatenate(
            [jnp.where(lead_slow, xl, xr_), jnp.where(lead_slow, xr_, xl)], axis=1))
        xh[0, rows, :] = hi
        xh[1, rows, :] = lo
        xt[:, rows] = hi.astype(F32).T.astype(BF16)
    sc, qc = pl.ds(0, H), pl.ds(H, H)

    def mixed(i, j):
        return dot(xt[i, :], xh[1, :, j])

    def square(i, j):
        return dot(xt[i, :], xh[0, :, j])

    left = xt[sc, :]
    cross = mixed(qc, sc).T + dot(
        jnp.concatenate([left, left], axis=1), jnp.concatenate([xh[1, :, qc], xh[0, :, qc]], axis=0)
    )
    for j in range(4):
        i0, j0 = 128 * (j // 2), 128 * (j % 2)
        (early if j < 2 else first[0]).put(j % 2, cross[i0 : i0 + 128, j0 : j0 + 128])
    pl.semaphore_wait(barrier, 10)
    first[0].scatter_y()
    early.scatter()
    above, on = upper()
    packed, diagonal = [], []
    for c, cols in enumerate((sc, qc)):
        m = mixed(cols, cols)
        g = square(cols, cols) + (m + m.T)
        first[1].put(c, g[:128, 128:])
        low = g[128:, 128:]
        first[2].put(c, jnp.where(above | on, g[:128, :128], low))
        diagonal.append(jnp.sum(jnp.where(on, low, 0.0), axis=0, keepdims=True))
    first[2].put_rows(jnp.concatenate(diagonal, axis=0))
    first[1].scatter_y()
    first[2].scatter_y()
    for c in first:
        c.scatter_z()
    early.swap()
    for c in first:
        c.gather_z()
    early.gather()
    for c in first:
        c.gather_y()

    sq = jnp.zeros((8, 128), F32)
    for j in range(4):
        part = early if j < 2 else first[0]
        if j % 2 == 0:
            part.arrive()
        i0, j0 = 128 * (j // 2), 128 * (j % 2)
        b = part.get(j % 2)
        sq = sq + norm(b, 2.0)
        a[i0 : i0 + 128, H + j0 : H + j0 + 128] = b
        a[H + j0 : H + j0 + 128, i0 : i0 + 128] = b.T
    first[1].arrive()
    for c, o in ((0, 0), (1, H)):
        b = first[1].get(c)
        sq = sq + norm(b, 2.0)
        a[o : o + 128, o + 128 : o + 256] = b
        a[o + 128 : o + 256, o : o + 128] = b.T
    first[2].arrive()
    for c, o in ((0, 0), (1, H)):
        b = first[2].get(c)
        t = b.T
        b0 = jnp.where(above | on, b, t)
        b2 = jnp.where(above, t, jnp.where(on, first[2].get_row(c), b))
        sq = sq + norm(b0, 1.0) + norm(b2, 1.0)
        a[o : o + 128, o : o + 128] = b0
        a[o + 128 : o + 256, o + 128 : o + 256] = b2
    scale = jnp.sqrt(jnp.sum(sq, keepdims=True) + EPS)
    inv = 1.0 / scale
    newton_schulz(a, ah, inv, a2, u, v, z2, z2h, yh)
    back = jnp.sqrt(ROWS / scale)

    def send(src, dst, i, to):
        c = pltpu.make_async_remote_copy(
            src_ref=src, dst_ref=dst, send_sem=xs.at[i], recv_sem=xr.at[i],
            device_id={"pair": to}, device_id_type=MESH,
        )
        c.start()
        return c

    top = 1.5 * z2[sc, :] - 0.5 * product(u, sc, yh)
    left = top[:, H:].T
    hi, lo = split(top[:, :H] * back)
    zh[0, sc, sc], zh[1, sc, sc] = hi, lo
    hi, lo = split(left * back)
    zh[0, qc, sc], zh[1, qc, sc] = hi, lo
    s_sent = []
    rest = []
    for i, rows in enumerate(tiles(R)):
        t = product(xh, rows, zh, sc)
        s_out[rows, :] = t[:, :128]
        s_sent.append(send(s_out.at[rows], s_in.at[rows], i, slow))
        rest.append(t[:, 128:])
    for i, rows in enumerate(tiles(W)):
        p_out[0, rows, :] = beside(rest[i], swap_halves(rest[i + 2]))
        p_out[1, rows, :] = beside(swap_halves(rest[i]), rest[i + 2])
    for c in range(2):
        s_sent.append(send(p_out.at[c], p_in.at[c], 4 + c, slow))
    low = 1.5 * z2[qc, qc] - 0.5 * product(u, qc, yh, qc)
    hi, lo = split(top[:, H:] * back)
    zh[0, sc, qc], zh[1, sc, qc] = hi, lo
    hi, lo = split(low * back)
    zh[0, qc, qc], zh[1, qc, qc] = hi, lo
    for rows in tiles(R):
        q_out[rows, :] = product(xh, rows, zh, qc)
    q_sent = send(q_out, q_in, 6, quick)

    keep(z2h, sc, top)
    keep(z2h, qc, jnp.concatenate([left, low], axis=1))
    for rows, t in zip(tiles(W), symmetric(z2h, ah)):
        keep(v, rows, t * inv)
    d_out[0] = product(z2h, sc, v, sc) * float(ROWS)
    d_out[1] = product(z2h, qc, v, qc) * float(ROWS)
    d_sent = [send(d_out.at[i], d_in.at[i], 7 + i, to) for i, to in ((0, slow), (1, quick))]

    q_sent.wait_recv()
    for rows in tiles(R):
        hi, lo = split(q_in[rows, :])
        nh[0, rows, H:] = hi
        nh[1, rows, H:] = lo
        qt[0, :, rows] = hi.astype(F32).T.astype(BF16)
        qt[1, :, rows] = lo.astype(F32).T.astype(BF16)
    cols = pl.ds(0, 128)
    for i, rows in enumerate(tiles(R)):
        s_sent[i].wait_recv()
        hi, lo = split(s_in[rows, :])
        nh[0, rows, cols] = hi
        nh[1, rows, cols] = lo
    g = dot(
        jnp.concatenate([qt[0], qt[0], qt[1]], axis=1),
        jnp.concatenate([nh[1, :, cols], nh[0, :, cols], nh[0, :, cols]], axis=0),
    )
    second[0].put(0, g[:128])
    second[0].put(1, g[128:])
    second[0].scatter()
    for c in range(2):
        s_sent[4 + c].wait_recv()
        hi, lo = split(p_in[c])
        parts = []
        for k in (pl.ds(0, W), pl.ds(W, W)):
            qh = qt[0, :, k]
            parts.append(dot(
                jnp.concatenate([qh, qh, qt[1, :, k]], axis=1), jnp.concatenate([lo, hi, hi], axis=0)
            ))
        g = parts[0] + swap_halves(parts[1])
        second[1 + c].put(0, beside(g[:128], swap_halves(g[128:])))
        second[1 + c].scatter()
    second[0].swap()
    second[1].swap()
    second[0].gather()
    second[1].gather()
    for i, rows in enumerate(tiles(W)):
        p0, p1 = p_in[0, rows, :], p_in[1, rows, :]
        keep(nh, rows, beside(p0, swap_halves(p1)), pl.ds(128, 128))
        keep(nh, pl.ds(W + i * T, T), beside(swap_halves(p0), p1), pl.ds(128, 128))
    second[2].swap()
    second[2].gather()
    for c in d_sent:
        c.wait_recv()
    sq = jnp.zeros((8, 128), F32)
    for i, o in ((0, 0), (1, H)):
        for rows in range(0, H, 128):
            b = d_in[i, rows : rows + 128, :]
            sq = sq + norm(b[:, :128], 1.0) + norm(b[:, 128:], 1.0)
            a[o + rows : o + rows + 128, o : o + H] = b
    def place(j, c, b):
        i0, j0 = H + 128 * j, 128 * c
        a[i0 : i0 + 128, j0 : j0 + 128] = b
        a[j0 : j0 + 128, i0 : i0 + 128] = b.T
        return norm(b, 2.0)

    second[0].arrive()
    for j in range(2):
        sq = sq + place(j, 0, second[0].get(j))
    for c in second[1:]:
        c.arrive()
    b0, b1 = second[1].get(0), second[2].get(0)
    sq = sq + place(0, 1, beside(b0, swap_halves(b1))) + place(1, 1, beside(swap_halves(b0), b1))
    scale = jnp.sqrt(jnp.sum(sq, keepdims=True) + EPS)
    inv = 1.0 / scale
    newton_schulz(a, ah, inv, a2, u, v, z2, z2h, yh)
    back = jnp.sqrt(ROWS / scale)
    top = (1.5 * z2[sc, :] - 0.5 * product(u, sc, yh)) * back
    low = (1.5 * z2[qc, qc] - 0.5 * product(u, qc, yh, qc)) * back
    keep(zn, sc, top)
    keep(zn, qc, jnp.concatenate([top[:, H:].T, low], axis=1))
    for c in s_sent + [q_sent] + d_sent:
        c.wait_send()
    for c in first + lines:
        c.drain()


def last(nh, zh, out_hbm, out, out_sem):
    odd = lax.rem(lax.axis_index("pair"), 2)
    s_cols = pl.ds(pl.multiple_of(odd * H, H), H)
    q_cols = pl.ds(pl.multiple_of((1 - odd) * H, H), H)
    stores = []
    for i in range(2):
        rows = pl.ds(W * i, W)
        t = product(nh, rows, zh)
        out[0, rows, :] = t[:, :H]
        out[1, rows, :] = t[:, H:]
        for k, cols in ((0, s_cols), (1, q_cols)):
            c = pltpu.make_async_copy(
                out.at[k, rows], out_hbm.at[rows, cols], out_sem.at[2 * i + k]
            )
            c.start()
            stores.append(c)
    for c in stores:
        c.wait()


def local(slab, moves):
    half = lambda *s: pltpu.VMEM(s, BF16)
    full = lambda *s: pltpu.VMEM(s, F32)
    bufs = []
    for nb, more in CHUNKS1:
        t = (8 * nb + more, 128)
        bufs += [full(2, 8, *t), full(8, *t), full(8, *t), full(8, *t), full(2, 8, *t)]
    for nb in (LINE1, *CHUNKS2):
        t = (nb, 16, 128)
        bufs += [full(8, *t), full(8, *t), full(*t), full(*t), full(8, *t)]
    dma = lambda *n: pltpu.SemaphoreType.DMA(n)
    n1, n2 = len(CHUNKS1), 1 + len(CHUNKS2)
    vmem = pl.BlockSpec(memory_space=pltpu.VMEM)
    new, root = pl.pallas_call(
        kernel,
        out_shape=[
            jax.ShapeDtypeStruct((2, R, W), BF16),
            jax.ShapeDtypeStruct((2, W, W), BF16),
        ],
        in_specs=[pl.BlockSpec(memory_space=pltpu.HBM), vmem],
        out_specs=[vmem, vmem],
        scratch_shapes=bufs
        + [
            full(R, W), half(2, R, W), half(W, R),
            full(W, W), half(2, W, W), full(W, W), half(2, W, W), half(2, W, W),
            full(W, W), half(2, W, W), half(2, W, W), half(2, W, W),
            full(2, H, H), full(2, H, H),
            full(R, 128), full(R, 128), full(2, W, 128), full(2, W, 128), full(R, H), full(R, H),
            half(2, H, R),
            dma(4), dma(n1, 4), dma(n1, 4), dma(n2, 3), dma(n2, 3), dma(9), dma(9),
        ],
        compiler_params=pltpu.CompilerParams(
            collective_id=1, has_side_effects=True, vmem_limit_bytes=50 * 2**20
        ),
    )(slab, moves)
    return pl.pallas_call(
        last,
        out_shape=jax.ShapeDtypeStruct((R, W), F32),
        in_specs=[vmem, vmem],
        out_specs=pl.BlockSpec(memory_space=pl.ANY),
        scratch_shapes=[full(2, R, H), dma(8)],
        compiler_params=pltpu.CompilerParams(vmem_limit_bytes=16 * 2**20),
    )(new, root)


def solution(mesh):
    placed = (P("row", "pair"), P(None, "pair"))
    return jax.shard_map(
        local, mesh=mesh, in_specs=placed, out_specs=P("row", "pair"), check_vma=False
    )
```
